32 devices in a mesh: tm: 4 (over y, x), tile: 8 (over z, core).
Axes of the slice: x: 2, y: 2, z: 4, core: 2. Of those that a mesh axis runs over, the one named last changes fastest.
Arguments:
- features: bfloat16 [8, 64, 16, 512], P('tm', None, 'tile'), may hold values from -6 to 6
- aligned: bfloat16 [8, 128, 16, 512], P('tm', None, 'tile'), may hold values from -6 to 6
- cotangent: bfloat16 [8, 64, 16, 512], P('tm', None, 'tile'), may hold values from -6 to 6
- weight: bfloat16 [9, 64, 192], replicated, may hold values from -0.15625 to 0.15625
- src_tile: int32 [8, 64, 2], P('tm', 'tile'), may hold values from 0 to 7, all different within a row; in each aligned block of 8 rows (0 to 7, 8 to 15, ..., all dimensions but the last counted through in order) at most 4 rows name the same one
- src_blk: int32 [8, 64, 2], P('tm', 'tile'), may hold values from 0 to 7
Outputs:
- grad_weight: float32 [9, 64, 192], replicated
- grad_feat: bfloat16 [8, 64, 16, 512], P('tm', None, 'tile')
- grad_prop: bfloat16 [8, 64, 16, 512], P('tm', None, 'tile')
The draws below stay inside these ranges and needn't reach their ends.
Inputs may be any that keep to these rules, and one draw needn't show every extreme that they name: `src_tile`: within one frame, the 8 blocks of one band name no source band more than 4 times over both orders, and the two orders of a block name different bands.
All inputs are finite; a program needn't handle non-finite values.
Results may differ from the reference program's by a relative error of at most 0.0057.
Values may be sent and summed in bfloat16 or wider, within the bound.
No kernel may reach another device: no remote copies, remote signals or barrier semaphores. Data moves between devices by JAX's collectives and lax.ppermute only.
A program may use at most 64 MiB of HBM per device.

```python
import math
import jax
import jax.numpy as jnp
import numpy as np
from jax import lax

C = 64
C3 = 192
W = 512
BPX = 128
TILES = 8
BLK = 8
NB = 64
CAP = 4
FRAMES = 8
H = 16


def set_ends(entries, stream_key, low, largest):
    extent = entries.shape
    place = [jax.random.randint(jax.random.fold_in(stream_key, axis), (), 0, extent[axis]) for axis in range(len(extent))]
    entries = entries.at[tuple(place)].set(low)
    longest = extent.index(max(extent))
    place[longest] = (place[longest] + 1) % extent[longest]
    return entries.at[tuple(place)].set(largest)


def level_of(stream_key, dims, split, smallest, high):
    def one(position, blocks):
        draws = jax.random.uniform(jax.random.fold_in(jax.random.fold_in(stream_key, 6), position), (blocks,), jnp.float32, smallest / len(split), high / len(split))
        return jnp.repeat(jnp.exp(draws), dims[position] // blocks).reshape((-1,) + (1,) * (len(dims) - position - 1))

    factor_of = one(*split[0])
    for cut in split[1:]:
        factor_of = factor_of * one(*cut)
    return factor_of


def routed_block(own_key, own, number, rows, number_of, top, bound, lean):
    order = jax.random.permutation(own_key, number_of)
    heavy_load, common = portions_of(number_of, rows * top, bound, lean, True), portions_of(number_of, rows * top, bound, lean, False)
    places = jnp.arange(number_of)

    def named(sizes, turn):
        used = int((sizes > 0).sum())
        fixed = max(1, used // 4)
        moved = fixed + (places - fixed + turn * (used - fixed)) % max(1, number_of - fixed)
        return jnp.zeros((number_of,), jnp.int32).at[order[jnp.where(places < fixed, places, moved)]].set(jnp.asarray(sizes, jnp.int32))

    sizes = jnp.where(number % 4 == 0, named(heavy_load, number // 4), named(common, number - number // 4 - 1))
    mixed = jax.random.permutation(jax.random.fold_in(own, 3), number_of)
    giver, sink = mixed[0:number_of // 2 * 2:2], mixed[1:number_of // 2 * 2:2]
    margin = jnp.minimum(sizes[giver] - 1, bound - sizes[sink]) // 2
    margin = jnp.where((giver == order[0]) | (sink == order[0]) | (sizes[sink] == 0), 0, jnp.maximum(margin, 0))
    moved = jax.random.randint(jax.random.fold_in(own, 4), (number_of // 2,), 0, 1 << 20) % (margin + 1)
    sizes = sizes.at[giver].add(-moved).at[sink].add(moved)
    items = jnp.searchsorted(jnp.cumsum(sizes), jnp.arange(rows * top), side="right").astype(jnp.int32)
    grid = items.reshape(top, rows).T
    grid = grid[jax.random.permutation(jax.random.fold_in(own, 1), rows)]
    turn = jax.random.randint(jax.random.fold_in(own, 2), (rows, 1), 0, top)
    return jnp.take_along_axis(grid, (jnp.arange(top)[None, :] + turn) % top, axis=1)


def portions_of(amount, total, reach, skew, full):
    loads = [(1 << 20) // math.isqrt(rank ** skew) + 1 for rank in range(1, amount + 1)]
    largest = reach if full else min(reach, max(-(-total // amount), total * loads[0] // sum(loads)))
    least = 1 if total - largest >= amount - 1 else 0
    counts, rest = [largest] + [least] * (amount - 1), total - largest - least * (amount - 1)
    while rest > 0:
        movable = [i for i in range(1, amount) if counts[i] < largest] or [i for i in range(1, amount) if counts[i] < reach]
        mass, remaining = sum([loads[i] for i in movable]), rest
        for i in movable:
            addition = min(reach - counts[i], max(1, remaining * loads[i] // mass), rest)
            counts[i] = counts[i] + addition
            rest = rest - addition
    return np.array(counts)


def bell_draw(stream_key, extent, scale, reach, pieces=(), held_as=jnp.bfloat16):
    array = jax.random.normal(stream_key, extent, jnp.float32) * scale
    if len(pieces) > 0:
        array = level_of(stream_key, extent, pieces, -0.22, 0.18) * array
    return jnp.clip(array, min=-reach, max=reach).astype(held_as)


def setup_inputs(seed: int = 0) -> dict:
    arg_keys = jax.random.split(jax.random.key(seed), 7)
    features = bell_draw(arg_keys[0], (FRAMES, C, H, W), 1.0, 6.0, ((0, 4), (2, 8)))
    aligned = bell_draw(arg_keys[1], (FRAMES, 2 * C, H, W), 1.0, 6.0, ((0, 4), (2, 8)))
    cotangent = bell_draw(arg_keys[2], (FRAMES, C, H, W), 1.0, 6.0, ((0, 4), (2, 8)))
    weight = bell_draw(arg_keys[3], (9, C, C3), (9 * C3) ** -0.5, 0.15625)
    src_tile_keys = jax.random.split(jax.random.fold_in(arg_keys[4], 1), FRAMES * NB // BLK)
    src_tile_turns = jax.random.permutation(jax.random.fold_in(arg_keys[4], 3), FRAMES * NB // BLK)
    src_tile = jax.vmap(lambda own, number: routed_block(jax.random.fold_in(arg_keys[4], 2), own, number, BLK, TILES, 2, CAP, 2))(src_tile_keys, src_tile_turns).reshape((FRAMES, NB, 2))
    src_blk = set_ends(jax.random.randint(arg_keys[5], (FRAMES, NB, 2), 0, BLK), jax.random.fold_in(arg_keys[5], 1), 0, BLK - 1).astype(jnp.int32)
    return dict(features=features, aligned=aligned, cotangent=cotangent, weight=weight, src_tile=src_tile, src_blk=src_blk)


def act_slope(preact):
    return 0.1 + 0.9 * jax.nn.sigmoid(preact)

def reference(features, aligned, cotangent, weight, src_tile, src_blk):
    weight_wide = weight.astype(jnp.float32)
    highest_precision = lax.Precision.HIGHEST

    def frame_grads(frame_items):
        feat_frame, align_frame, cot_frame = frame_items
        inputs = jnp.concatenate((feat_frame, align_frame), axis=0).astype(jnp.float32)
        padded_input = jnp.pad(inputs, ((0, 0), (1, 1), (1, 1)))
        preact = jnp.zeros((C, H, W), jnp.float32)
        for row_tap in range(3):
            for col_tap in range(3):
                window = padded_input[:, row_tap:row_tap + H, col_tap:col_tap + W]
                preact = preact + jnp.einsum('oi,irc->orc', weight_wide[3 * row_tap + col_tap], window, precision=highest_precision)
        cot_pre = (cot_frame.astype(jnp.float32) * act_slope(preact)).astype(jnp.bfloat16)
        cot_wide = cot_pre.astype(jnp.float32)
        padded_cot = jnp.pad(cot_wide, ((0, 0), (1, 1), (1, 1)))
        summed = jnp.zeros((C3, H, W), jnp.float32)
        term_list = []
        for row_tap in range(3):
            for col_tap in range(3):
                window = padded_cot[:, 2 - row_tap:2 - row_tap + H, 2 - col_tap:2 - col_tap + W]
                summed = summed + jnp.einsum('oi,orc->irc', weight_wide[3 * row_tap + col_tap], window, precision=highest_precision)
                source_win = padded_input[:, row_tap:row_tap + H, col_tap:col_tap + W]
                term_list.append(jnp.einsum('orc,irc->oi', cot_wide, source_win, precision=highest_precision))
        return (summed.astype(jnp.bfloat16), jnp.stack(term_list))
    input_grads, frame_weights = lax.map(frame_grads, (features, aligned, cotangent))
    grad_weight = lax.optimization_barrier(jnp.sum(frame_weights, axis=0)) * (1.0 / math.sqrt(FRAMES * H * W))
    grad_feat = input_grads[:, :C]
    aligned_grads = input_grads[:, C:].reshape(FRAMES, 2, C, NB, BPX)
    source_frames = (src_tile * BLK + src_blk).astype(jnp.int32)

    def one_target(target):
        summed = jnp.zeros((NB, C, BPX), jnp.float32)
        for order in range(2):
            source = target + 1 + order
            valid = (source < FRAMES).astype(jnp.float32)
            clipped = jnp.minimum(source, FRAMES - 1).astype(jnp.int32)
            blocks = jnp.transpose(aligned_grads[clipped, order].astype(jnp.float32), (1, 0, 2)) * valid
            summed = summed.at[source_frames[clipped, :, order]].add(blocks)
        return jnp.transpose(summed, (1, 0, 2)).reshape(C, H, W).astype(jnp.bfloat16)
    grad_prop = lax.map(one_target, jnp.arange(FRAMES, dtype=jnp.int32))
    return (grad_weight, grad_feat, grad_prop)
```

```python
import math

import jax
import jax.numpy as jnp
from jax import lax
from jax.experimental import pallas as pl
from jax.experimental.pallas import tpu as pltpu
from jax.sharding import PartitionSpec as P

F32 = jnp.float32
BF16 = jnp.bfloat16


def act_slope(preact):
    return 0.1 + 0.9 * jax.nn.sigmoid(preact)


TABLE_ROWS = 16


def full(memory_space=pltpu.VMEM):
    return pl.BlockSpec(memory_space=memory_space)


def call(kernel, out_shapes, args, scalars, scratch=(), flops=0, nbytes=1 << 20):
    specs = [full(pltpu.SMEM)] * scalars + [full()] * (len(args) - scalars)
    return pl.pallas_call(
        kernel,
        out_shape=out_shapes,
        in_specs=specs,
        out_specs=[full()] * len(out_shapes),
        scratch_shapes=list(scratch),
        cost_estimate=pl.CostEstimate(flops=flops, bytes_accessed=nbytes, transcendentals=0),
        compiler_params=pltpu.CompilerParams(vmem_limit_bytes=48 << 20),
    )(*args)


def from_left(values):
    lane = lax.broadcasted_iota(jnp.int32, values.shape, 1)
    return jnp.where(lane == 0, 0.0, pltpu.roll(values, 1, 1))


def from_right(values):
    columns = values.shape[1]
    lane = lax.broadcasted_iota(jnp.int32, values.shape, 1)
    return jnp.where(lane == columns - 1, 0.0, pltpu.roll(values, columns - 1, 1))


def taps_of(row):
    wide = row.astype(F32)
    return (from_right(wide).astype(BF16), row, from_left(wide).astype(BF16))


def forward_kernel(pos, u, rin, rout, cot, w3, tab, msg0, msg1, g3, edge, halo):
    core = pos[0]
    ch = cot.shape[2]
    halo[core] = rout[...]
    halo[1 - core] = rin[...]
    for f, msg in ((0, msg0), (1, msg1)):
        rows = (halo.at[0, f], u.at[f, 0], u.at[f, 1], halo.at[1, f])
        for r in range(2):
            taps = jnp.dot(w3[0], rows[r][...], preferred_element_type=F32)
            taps += jnp.dot(w3[1], rows[r + 1][...], preferred_element_type=F32)
            taps += jnp.dot(w3[2], rows[r + 2][...], preferred_element_type=F32)
            z = taps[ch : 2 * ch] + from_left(taps[:ch]) + from_right(taps[2 * ch :])
            g = (cot[f, r].astype(F32) * act_slope(z)).astype(BF16)
            msg[r * ch : (r + 1) * ch] = g
            for k, part in enumerate(taps_of(g)):
                g3[f, r, k * ch : (k + 1) * ch] = part
            if f == 0:

                @pl.when(core == r)
                def _():
                    edge[...] = g

        msg[2 * ch :] = tab[f]


def taps_kernel(pos, u, rin, rout, g3, keep, send, halo, total):
    core = pos[0]
    size = g3.shape[2]
    half = keep.shape[0]
    halo[core] = rout[...]
    halo[1 - core] = rin[...]
    for ky in range(3):
        acc = jnp.zeros((size, u.shape[2]), F32)
        for f in range(2):
            rows = (halo.at[0, f], u.at[f, 0], u.at[f, 1], halo.at[1, f])
            for r in range(2):
                acc += lax.dot_general(
                    g3[f, r], rows[r + ky][...], (((1,), (1,)), ((), ())), preferred_element_type=F32
                )
        total[ky * size : (ky + 1) * size] = acc
    keep[...] = total[pl.ds(pl.multiple_of(core * half, 8), half)]
    send[...] = total[pl.ds(pl.multiple_of((1 - core) * half, 8), half)]


def shares_kernel(pos, keep, got, own, *others):
    group = pos[2]
    part = own.shape[0]
    for k, out in enumerate((own, *others)):
        at = pl.ds(pl.multiple_of((group ^ k) * part, 8), part)
        out[...] = keep[at] + got[at]


def assemble_kernel(pos, mine, theirs, out):
    core, group = pos[0], pos[2]
    part = mine.shape[1]
    parts = mine.shape[0]
    for source, side in ((mine, core), (theirs, 1 - core)):
        for k in range(parts):
            at = (side * parts + (group ^ k)) * part
            out[pl.ds(pl.multiple_of(at, 8), part)] = source[k]


def collect(pos, own, near, far, g3, tabs):
    core, chip, chips = pos[0], pos[1], len(near) + 1
    ch = g3.shape[1] // 3
    step = 1 - 2 * core
    entries = [(own, chip, core)]
    entries += [(ref, chip - step * (k + 1), core) for k, ref in enumerate(near)]
    entries += [(ref, chip + step * (k + 1), 1 - core) for k, ref in enumerate(far)]
    zero = jnp.zeros(g3.shape[1:], BF16)
    g3[0] = zero
    g3[g3.shape[0] - 1] = zero
    for ref, where, first in entries:

        @pl.when((where >= 0) & (where < chips))
        def _(ref=ref, where=where, first=first):
            for h in range(2):
                band = 2 * where + (first if h == 0 else 1 - first)
                for r in range(2):
                    row = 2 * band + r + 1
                    for k, part in enumerate(taps_of(ref[h, r * ch : (r + 1) * ch])):
                        g3[row, k * ch : (k + 1) * ch] = part
                codes = ref[h, 2 * ch : 2 * ch + TABLE_ROWS, :128].astype(F32).astype(jnp.int32)
                tabs[pl.ds(band, 1)] = codes[:1]


def spread(me, g3, wt, codes, gu, first, second):
    ch = wt.shape[0] // 2
    size = g3.shape[1]
    columns = g3.shape[2]

    def one_row(r, _):
        window = g3[pl.ds(r, 3)].reshape(3 * size, columns)
        gu[...] = jnp.dot(wt[...], window, preferred_element_type=F32).astype(BF16).astype(F32)
        for j in range(4):
            for q, sums in ((0, first), (1, second)):
                code = codes[r // 2, ((r % 2) * 4 + j) * 2 + q]

                @pl.when(code // 8 == me)
                def _(j=j, q=q, sums=sums, code=code):
                    sums[code % 8] += gu[q * ch : (q + 1) * ch, 128 * j : 128 * (j + 1)]

        return 0

    lax.fori_loop(0, g3.shape[0] - 2, one_row, 0)


def earlier_kernel(chips, pos, *refs):
    n = chips - 1
    own, near, far = refs[0], refs[1 : 1 + n], refs[1 + n : 1 + 2 * n]
    msg0, other0, zhalo, wt = refs[1 + 2 * n : 5 + 2 * n]
    local, passed, feat, g3, rows4, tabs, codes, gu, acc, sem = refs[5 + 2 * n :]
    core, chip = pos[0], pos[1]
    me = 2 * chip + core
    ch = local.shape[1]
    size = 3 * ch
    collect(pos, own, near, far, g3, tabs)
    copy = pltpu.make_async_copy(tabs, codes, sem)
    copy.start()
    local[...] = jnp.zeros(local.shape, F32)
    acc[...] = jnp.zeros(acc.shape, F32)
    columns = g3.shape[2]
    for k, part in enumerate(taps_of(zhalo[...])):
        rows4[3 * core, k * ch : (k + 1) * ch] = part
    for k, part in enumerate(taps_of(other0[pl.ds(pl.multiple_of(core * ch, ch), ch)])):
        rows4[3 * (1 - core), k * ch : (k + 1) * ch] = part
    for r in range(2):
        for k, part in enumerate(taps_of(msg0[r * ch : (r + 1) * ch])):
            rows4[1 + r, k * ch : (k + 1) * ch] = part
    for r in range(2):
        window = rows4[r : r + 3].reshape(3 * size, columns)
        feat[0, r] = jnp.dot(wt[:ch], window, preferred_element_type=F32).astype(BF16)
        window = g3[pl.ds(2 * me + r, 3)].reshape(3 * size, columns)
        feat[1, r] = jnp.dot(wt[:ch], window, preferred_element_type=F32).astype(BF16)
    copy.wait()
    spread(me, g3, wt.at[ch:], codes, gu, local, acc)
    passed[...] = acc[...].astype(BF16)


def later_kernel(chips, pos, *refs):
    n = chips - 1
    own, near, far = refs[0], refs[1 : 1 + n], refs[1 + n : 1 + 2 * n]
    local, passed, wt = refs[1 + 2 * n : 4 + 2 * n]
    prop, g3, tabs, codes, gu, sums0, sums1, sem = refs[4 + 2 * n :]
    core, chip = pos[0], pos[1]
    me = 2 * chip + core
    ch = local.shape[1]
    collect(pos, own, near, far, g3, tabs)
    copy = pltpu.make_async_copy(tabs, codes, sem)
    copy.start()
    sums0[...] = local[...]
    sums1[...] = passed[...].astype(F32)
    copy.wait()
    spread(me, g3, wt.at[ch:], codes, gu, sums1, sums0)
    for s, sums in ((0, sums0), (1, sums1)):
        for b in range(8):
            j = b % 4
            prop[s, b // 4, :, 128 * j : 128 * (j + 1)] = sums[b].astype(BF16)


def total_over(parts):
    first = parts[0]
    for part in parts[1:]:
        first = first + part
    return first


def few_bands(features, aligned, cotangent, weight, src_tile, src_blk):
    frames, channels, height, columns = features.shape
    inner = channels + aligned.shape[1]
    tiles = lax.axis_size("tile")
    groups = lax.axis_size("tm")
    chips = tiles // 2
    tile = lax.axis_index("tile")
    group = lax.axis_index("tm")
    core = tile % 2
    pos = jnp.stack([core, tile // 2, group]).astype(jnp.int32)

    cores = [(i, i ^ 1) for i in range(tiles)]
    joints = [(2 * z + 1, 2 * z + 2) for z in range(chips - 1)]
    joints += [(b, a) for a, b in joints]

    def along(k, targets=None):
        route = []
        for z in range(chips - k):
            route += [(2 * z, 2 * z + 2 * k), (2 * z + 2 * k + 1, 2 * z + 1)]
        return [(a, b) for a, b in route if targets is None or b // 2 in targets]

    def to_tile(block, route):
        return lax.ppermute(block, "tile", route)

    def to_group(block, route):
        return lax.ppermute(block, "tm", route)

    def row_of(r):
        return jnp.concatenate(
            [lax.dynamic_slice_in_dim(x, r, 1, axis=2)[:, :, 0] for x in (features, aligned)], axis=1
        )

    rout = to_tile(row_of(core), joints)
    rin = to_tile(row_of(1 - core), cores)
    u = jnp.transpose(jnp.concatenate((features, aligned), axis=1), (0, 2, 1, 3))
    cot = jnp.transpose(cotangent, (0, 2, 1, 3))
    w3 = weight.reshape(3, 3 * channels, inner)
    wt = jnp.transpose(weight.reshape(3, 3 * channels, inner)[::-1].reshape(9 * channels, inner))
    codes = (src_tile * 8 + src_blk).reshape(frames, 1, -1).astype(BF16)
    tab = jnp.pad(codes, ((0, 0), (0, TABLE_ROWS - 1), (0, columns - codes.shape[2])))

    halo = pltpu.VMEM((2, frames, inner, columns), BF16)
    msg_shape = jax.ShapeDtypeStruct((2 * channels + TABLE_ROWS, columns), BF16)
    msg0, msg1, g3, edge = call(
        forward_kernel,
        [
            msg_shape,
            msg_shape,
            jax.ShapeDtypeStruct((frames, 2, 3 * channels, columns), BF16),
            jax.ShapeDtypeStruct((channels, columns), BF16),
        ],
        (pos, u, rin, rout, cot, w3, tab),
        1,
        [halo],
        flops=10**9,
        nbytes=4 << 20,
    )

    def gathered(block):
        near = [None] * (chips - 1)
        for k in (1, 0):
            near[k] = to_tile(block, along(k + 1))
        near[2] = to_tile(near[1], along(1, (0, chips - 1)))
        return near, [to_tile(x, cores) for x in near]

    other1 = to_tile(msg1, cores)
    own1 = jnp.stack((msg1, other1))
    near1, far1 = gathered(own1)
    other0 = to_tile(msg0, cores)
    zhalo = to_tile(edge, joints)
    back = [(m + 1, m) for m in range(groups - 1)]
    own0 = to_group(jnp.stack((msg0, other0)), back)
    near0, far0 = gathered(own0)

    part_rows = 9 * channels // (2 * groups)
    half_shape = jax.ShapeDtypeStruct((9 * channels // 2, inner), F32)
    keep, send = call(
        taps_kernel,
        [half_shape, half_shape],
        (pos, u, rin, rout, g3),
        1,
        [halo, pltpu.VMEM((9 * channels, inner), F32)],
        flops=10**9,
        nbytes=4 << 20,
    )
    got = to_tile(send, cores)
    part_shape = jax.ShapeDtypeStruct((part_rows, inner), F32)
    shares = call(shares_kernel, [part_shape] * groups, (pos, keep, got), 1)
    swaps = [[(i, i ^ k) for i in range(groups)] for k in range(groups)]
    share = total_over([shares[0]] + [to_group(shares[k], swaps[k]) for k in range(1, groups)])
    turns = [[(2 * z + c, 2 * (z ^ k) + c) for z in range(chips) for c in range(2)] for k in range(chips)]
    share = total_over([share] + [to_tile(share, turns[k]) for k in range(1, chips)])
    pixels = frames * groups * height * tiles * columns
    share = share * (1.0 / math.sqrt(pixels))
    mine = jnp.stack([share] + [to_group(share, swaps[k]) for k in range(1, groups)])
    theirs = to_tile(mine, cores)
    (grad_weight,) = call(
        assemble_kernel, [jax.ShapeDtypeStruct((9 * channels, inner), F32)], (pos, mine, theirs), 1
    )

    bands = 2 * chips
    sums_shape = (8, channels, 128)
    work = [
        pltpu.VMEM((2 * bands + 2, 3 * channels, columns), BF16),
        pltpu.VMEM((bands, 128), jnp.int32),
        pltpu.SMEM((bands, 128), jnp.int32),
        pltpu.VMEM((2 * channels, columns), F32),
        pltpu.VMEM(sums_shape, F32),
    ]
    rows4 = pltpu.VMEM((4, 3 * channels, columns), BF16)
    local, passed, feat = call(
        lambda *refs: earlier_kernel(chips, *refs),
        [
            jax.ShapeDtypeStruct(sums_shape, F32),
            jax.ShapeDtypeStruct(sums_shape, BF16),
            jax.ShapeDtypeStruct((frames, 2, channels, columns), BF16),
        ],
        (pos, own1, *near1, *far1, msg0, other0, zhalo, wt),
        1,
        work[:1] + [rows4] + work[1:] + [pltpu.SemaphoreType.DMA],
        flops=3 * 10**9,
        nbytes=8 << 20,
    )
    passed = to_group(passed, back)
    (prop,) = call(
        lambda *refs: later_kernel(chips, *refs),
        [jax.ShapeDtypeStruct((2, 2, channels, columns), BF16)],
        (pos, own0, *near0, *far0, local, passed, wt),
        1,
        work + [pltpu.VMEM(sums_shape, F32), pltpu.SemaphoreType.DMA],
        flops=3 * 10**9,
        nbytes=8 << 20,
    )
    return (
        grad_weight.reshape(9, channels, inner),
        jnp.transpose(feat, (0, 2, 1, 3)),
        jnp.transpose(prop, (0, 2, 1, 3)),
    )


def with_halo(cells, sides, width):
    for axis, dim in sides:
        count = lax.axis_size(axis)
        ends = count - 1
        head = lax.slice_in_dim(cells, 0, width, axis=dim)
        tail = lax.slice_in_dim(cells, cells.shape[dim] - width, cells.shape[dim], axis=dim)
        cells = jnp.concatenate(
            [
                lax.ppermute(tail, axis, [(i, (i + 1) % count) for i in range(ends)]),
                cells,
                lax.ppermute(head, axis, [((i + 1) % count, i) for i in range(ends)]),
            ],
            axis=dim,
        )
    return cells


def passed_along(block, axis, distance):
    devices = range(lax.axis_size(axis))
    route = [(i - distance, i) for i in devices if i - distance in devices]
    return lax.ppermute(block, axis, route)


def pad_columns(values):
    return jnp.pad(values, ((0, 0), (0, 0), (0, 0), (1, 1)))


def conv_forward(weight, padded_input, height):
    columns = padded_input.shape[3] - 2
    summed = jnp.zeros((padded_input.shape[0], weight.shape[1], height, columns), jnp.float32)
    for row_tap in range(3):
        for col_tap in range(3):
            window = padded_input[:, :, row_tap : row_tap + height, col_tap : col_tap + columns]
            summed = summed + jnp.einsum(
                "oi,firc->forc",
                weight[3 * row_tap + col_tap],
                window,
                preferred_element_type=jnp.float32,
            )
    return summed


def conv_transpose(weight, padded_input, height):
    columns = padded_input.shape[3] - 2
    summed = jnp.zeros((padded_input.shape[0], weight.shape[2], height, columns), jnp.float32)
    for row_tap in range(3):
        for col_tap in range(3):
            window = padded_input[
                :, :, 2 - row_tap : 2 - row_tap + height, 2 - col_tap : 2 - col_tap + columns
            ]
            summed = summed + jnp.einsum(
                "oi,forc->firc",
                weight[3 * row_tap + col_tap],
                window,
                preferred_element_type=jnp.float32,
            )
    return summed.astype(jnp.bfloat16)


def weight_grad(padded_input, cot_pre):
    height = cot_pre.shape[2]
    columns = cot_pre.shape[3]
    term_list = []
    for row_tap in range(3):
        for col_tap in range(3):
            window = padded_input[:, :, row_tap : row_tap + height, col_tap : col_tap + columns]
            term_list.append(
                jnp.einsum("forc,firc->oi", cot_pre, window, preferred_element_type=jnp.float32)
            )
    return jnp.stack(term_list)


def build_slots(aligned_grad, tiles, blocks, tile_count, capacity):
    frames, stacked, height, columns = aligned_grad.shape
    block_count = tiles.shape[1]
    pixels = height * columns // block_count
    pieces = aligned_grad.reshape(frames, 2, stacked // 2, block_count, pixels)
    row_ids = jnp.arange(2 * block_count, dtype=jnp.int32)
    destination = jnp.swapaxes(tiles, 1, 2).reshape(frames, 2 * block_count)
    target_code = (
        jnp.swapaxes(blocks, 1, 2).reshape(frames, 2 * block_count)
        + (row_ids // block_count * block_count)[None, :]
    )
    tile_hit_count = (
        destination[:, :, None] == jnp.arange(tile_count, dtype=jnp.int32)[None, None, :]
    ).astype(jnp.int32)
    earlier = jnp.cumsum(tile_hit_count, axis=1) - tile_hit_count
    slot_ids = destination * capacity + jnp.sum(tile_hit_count * earlier, axis=2)
    source_selector = (
        slot_ids[:, None, :] == jnp.arange(tile_count * capacity, dtype=jnp.int32)[None, :, None]
    ).astype(jnp.bfloat16)
    target_onehot = (target_code[:, :, None] == row_ids[None, None, :]).astype(jnp.bfloat16)
    placing = jnp.einsum(
        "anu,auo->ano", source_selector, target_onehot, preferred_element_type=jnp.float32
    ).astype(jnp.bfloat16)
    select_split = source_selector.reshape(frames, tile_count * capacity, 2, block_count)
    payload = jnp.einsum(
        "fsob,focbp->fscp", select_split, pieces, preferred_element_type=jnp.float32
    ).astype(jnp.bfloat16)
    return (payload, placing)


def place_blocks(received):
    payload, placing = received
    return jnp.einsum("fsb,fscp->fcbp", placing, payload, preferred_element_type=jnp.float32)


def deliver(aligned_grad, tiles, blocks, tile_count, capacity):
    payload, placing = build_slots(aligned_grad, tiles, blocks, tile_count, capacity)
    return place_blocks(
        (
            lax.all_to_all(payload, "tile", split_axis=1, concat_axis=1, tiled=True),
            lax.all_to_all(placing, "tile", split_axis=1, concat_axis=1, tiled=True),
        )
    )


def many_bands(features, aligned, cotangent, weight, src_tile, src_blk):
    frames, channels, height, columns = features.shape
    inputs = jnp.concatenate((features, aligned), axis=1)
    padded_in = pad_columns(with_halo(inputs, (("tile", 2),), 1))
    preact = conv_forward(weight, padded_in, height)
    cot_pre = (cotangent * act_slope(preact)).astype(jnp.bfloat16)
    padded_cot = pad_columns(with_halo(cot_pre, (("tile", 2),), 1))
    tile_count = lax.axis_size("tile")
    block_count = src_tile.shape[1]
    capacity = max(2, (4 * block_count + tile_count - 1) // tile_count)
    input_grad = conv_transpose(weight, padded_cot, height)
    local_weight = weight_grad(padded_in, cot_pre)
    feat_grad = input_grad[:, :channels]
    aligned_grad = input_grad[:, channels:]
    arrived = deliver(aligned_grad, src_tile, src_blk, tile_count, capacity)
    landed = arrived.reshape(frames, channels, 2, height, columns)
    extended = jnp.pad(landed[:, :, 0], ((1, 1), (0, 0), (0, 0), (0, 0))) + jnp.pad(
        landed[:, :, 1], ((0, 2), (0, 0), (0, 0), (0, 0))
    )
    arriving = passed_along(extended[:2], "tm", -1)
    resident = extended[2:]
    resident = jnp.concatenate((resident[: frames - 2], resident + arriving), axis=0)
    total_weight = lax.psum(local_weight, ("tm", "tile"))
    pixels = frames * lax.axis_size("tm") * height * tile_count * columns
    grad_weight = total_weight * (1.0 / math.sqrt(pixels))
    return (grad_weight, feat_grad, resident.astype(jnp.bfloat16))


def solution(mesh):
    in_specs = (
        P("tm", None, "tile", None),
        P("tm", None, "tile", None),
        P("tm", None, "tile", None),
        P(),
        P("tm", "tile", None),
        P("tm", "tile", None),
    )
    out_specs = (P(), P("tm", None, "tile", None), P("tm", None, "tile", None))
    few = mesh.shape["tile"] == 8 and mesh.shape["tm"] == 4
    body = few_bands if few else many_bands
    return jax.shard_map(body, mesh=mesh, in_specs=in_specs, out_specs=out_specs, check_vma=False)
```

```python
import math

import jax
import jax.numpy as jnp
from jax import lax
from jax.experimental import pallas as pl
from jax.experimental.pallas import tpu as pltpu
from jax.sharding import PartitionSpec as P

F32 = jnp.float32
BF16 = jnp.bfloat16


def act_slope(preact):
    return 0.1 + 0.9 * jax.nn.sigmoid(preact)


TABLE_ROWS = 16
LANES = 128


def full(memory_space=pltpu.VMEM):
    return pl.BlockSpec(memory_space=memory_space)


def call(kernel, out_shapes, args, scalars, scratch=(), micros=1.0):
    specs = [full(pltpu.SMEM)] * scalars + [full()] * (len(args) - scalars)
    return pl.pallas_call(
        kernel,
        out_shape=out_shapes,
        in_specs=specs,
        out_specs=[full()] * len(out_shapes),
        scratch_shapes=list(scratch),
        cost_estimate=pl.CostEstimate(flops=int(micros * 1000000000.0), bytes_accessed=0, transcendentals=0),
        compiler_params=pltpu.CompilerParams(vmem_limit_bytes=24 << 20),
    )(*args)


def after(value, *others):
    return lax.optimization_barrier((value, *others))[0]


def from_left(values):
    lane = lax.broadcasted_iota(jnp.int32, values.shape, 1)
    return jnp.where(lane == 0, 0.0, pltpu.roll(values, 1, 1))


def from_right(values):
    columns = values.shape[1]
    lane = lax.broadcasted_iota(jnp.int32, values.shape, 1)
    return jnp.where(lane == columns - 1, 0.0, pltpu.roll(values, columns - 1, 1))


def taps_of(row):
    wide = row.astype(F32)
    return (from_right(wide).astype(BF16), row, from_left(wide).astype(BF16))


def forward_kernel(pos, u, rin, rout, cot, w3, tab, msg, g3, halo):
    core = pos[0]
    frames, _, ch, columns = cot.shape
    pieces = columns // LANES
    halo[core] = rout[...]
    halo[1 - core] = rin[...]
    for f in range(frames):
        rows = (halo.at[0, f], u.at[f, 0], u.at[f, 1], halo.at[1, f])
        for r in range(2):
            taps = jnp.dot(w3[0], rows[r][...], preferred_element_type=F32)
            taps += jnp.dot(w3[1], rows[r + 1][...], preferred_element_type=F32)
            taps += jnp.dot(w3[2], rows[r + 2][...], preferred_element_type=F32)
            z = taps[ch : 2 * ch] + from_left(taps[:ch]) + from_right(taps[2 * ch :])
            g = (cot[f, r].astype(F32) * act_slope(z)).astype(BF16)
            for j in range(pieces):
                at = ((2 * f + r) * pieces + j) * ch
                msg[at : at + ch] = g[:, LANES * j : LANES * (j + 1)]
            for k, part in enumerate(taps_of(g)):
                g3[f, r, k * ch : (k + 1) * ch] = part
    msg[2 * frames * pieces * ch :] = tab[...]


def taps_kernel(pos, u, rin, rout, g3, w3, keep, send, wa, wf, halo, total):
    core = pos[0]
    size = g3.shape[2]
    half = keep.shape[0]
    halo[core] = rout[...]
    halo[1 - core] = rin[...]
    for ky in range(3):
        acc = jnp.zeros((size, u.shape[2]), F32)
        for f in range(u.shape[0]):
            rows = (halo.at[0, f], u.at[f, 0], u.at[f, 1], halo.at[1, f])
            for r in range(2):
                acc += lax.dot_general(
                    g3[f, r], rows[r + ky][...], (((1,), (1,)), ((), ())), preferred_element_type=F32
                )
        total[ky * size : (ky + 1) * size] = acc
    keep[...] = total[pl.ds(pl.multiple_of(core * half, 8), half)]
    send[...] = total[pl.ds(pl.multiple_of((1 - core) * half, 8), half)]
    ch = size // 3
    for kx in range(3):
        rows = [w3[ky, kx * ch : (kx + 1) * ch] for ky in (2, 1, 0)]
        turned = jnp.transpose(jnp.concatenate(rows, axis=0).astype(F32)).astype(BF16)
        wf[kx * ch : (kx + 1) * ch] = turned[:ch]
        wa[2 * kx * ch : 2 * (kx + 1) * ch] = turned[ch:]


def shares_kernel(pos, keep, got, own, *others):
    group = pos[2]
    part = own.shape[0]
    for k, out in enumerate((own, *others)):
        at = pl.ds(pl.multiple_of((group ^ k) * part, 8), part)
        out[...] = keep[at] + got[at]


def assemble_kernel(pos, mine, theirs, out):
    core, group = pos[0], pos[2]
    part = mine.shape[1]
    parts = mine.shape[0]
    for source, side in ((mine, core), (theirs, 1 - core)):
        for k in range(parts):
            at = (side * parts + (group ^ k)) * part
            out[pl.ds(pl.multiple_of(at, 8), part)] = source[k]


def collect(pos, entries, chips, g, tabs):
    core = pos[0]
    frames, _, ch, columns = g.shape
    pieces = columns // LANES
    for ref, where, first in entries:

        @pl.when((where >= 0) & (where < chips))
        def _(ref=ref, where=where, first=first):
            for h in range(2):
                band = 2 * where + (first if h == 0 else 1 - first)
                for f in range(frames):
                    for r in range(2):
                        for j in range(pieces):
                            at = ((2 * f + r) * pieces + j) * ch
                            lanes = slice(LANES * j, LANES * (j + 1))
                            g[f, 2 * band + r + 1, :, lanes] = ref[h, at : at + ch]
                codes = ref[h, 2 * frames * pieces * ch :].astype(F32).astype(jnp.int32)
                tabs[pl.ds(band, 1)] = codes[:1]


def convolved(weights, window):
    taps = jnp.dot(weights[...], window, preferred_element_type=F32)
    size = taps.shape[0] // 3
    total = taps[size : 2 * size] + from_right(taps[:size]) + from_left(taps[2 * size :])
    return total.astype(BF16)


def spread(low, high, me, g, weights, codes, hits, gu, sums):
    frames, _, ch, columns = g.shape
    pieces = columns // LANES

    def one_row(r, count):
        for f in range(frames):
            value = convolved(weights, g[f, pl.ds(r, 3)].reshape(3 * ch, columns))
            for j in range(pieces):
                for q in range(2):
                    gu[f, r, j, q] = value[q * ch : (q + 1) * ch, LANES * j : LANES * (j + 1)]
            for k in range(2 * pieces):
                lane = (2 * f + r % 2) * (2 * pieces) + k
                hits[count] = (r // 2) * LANES + lane
                count += (lax.shift_right_logical(codes[r // 2, lane], 3) == me).astype(jnp.int32)
        return count

    count = lax.fori_loop(low, high, one_row, 0)

    def one_hit(k, _):
        hit = hits[k]
        band, lane = hit // LANES, hit % LANES
        f, block, q = lane // (4 * pieces), (lane % (4 * pieces)) // 2, lane % 2
        target = codes[band, lane] % 8
        sums[f + 1 - q, target] += gu[f, 2 * band + block // pieces, block % pieces, q].astype(F32)
        return 0

    lax.fori_loop(0, count, one_hit, 0)


def ready_rows(chip, reach, chips):
    low, high = jnp.maximum(chip - reach, 0), jnp.minimum(chip + reach, chips - 1)
    return 4 * low + (low > 0).astype(jnp.int32), 4 * high + 4 - (high < chips - 1).astype(jnp.int32)


def stage_kernel(reach, chips, pos, *refs):
    core, chip = pos[0], pos[1]
    me = 2 * chip + core
    step = 1 - 2 * core
    if reach == 1:
        own, near, far, wa, wf, sums, feat, g, tabs, codes, hits, gu, sem = refs
        entries = [(own, chip, core)]
        sums[...] = jnp.zeros(sums.shape, F32)
    else:
        near0, far0, near, far, wa, sums_in, sums, g, tabs, codes, hits, gu, sem = refs
        entries = [(near0, chip - step * (reach - 1), core), (far0, chip + step * (reach - 1), 1 - core)]
        sums[...] = sums_in[...]
    entries += [(near, chip - step * reach, core), (far, chip + step * reach, 1 - core)]
    frames, rows, ch, columns = g.shape
    zero = jnp.zeros((ch, columns), BF16)
    for f in range(frames):
        g[f, 0] = zero
        g[f, rows - 1] = zero
    collect(pos, entries, chips, g, tabs)
    copy = pltpu.make_async_copy(tabs, codes, sem)
    copy.start()
    if reach == 1:
        for f in range(frames):
            for r in range(2):
                feat[f, r] = convolved(wf, g[f, pl.ds(2 * me + r, 3)].reshape(3 * ch, columns))
    copy.wait()
    low, high = ready_rows(chip, reach, chips)
    if reach == 1:
        spread(low, high, me, g, wa, codes, hits, gu, sums)
    else:
        old_low, old_high = ready_rows(chip, reach - 1, chips)
        spread(low, old_low, me, g, wa, codes, hits, gu, sums)
        spread(old_high, high, me, g, wa, codes, hits, gu, sums)


def final_stage_kernel(reach, chips, pos, near0, far0, near, far, wa, sums_in, passed, local, sums, *work):
    stage_kernel(reach, chips, pos, near0, far0, near, far, wa, sums_in, sums, *work)
    for s in range(2):
        passed[s] = sums[s].astype(BF16)
    local[...] = sums[2]


def last_kernel(passed, local, prop):
    ch = local.shape[1]
    pieces = prop.shape[3] // LANES
    for s in range(2):
        for b in range(2 * pieces):
            j = b % pieces
            value = passed[s, b]
            if s == 0:
                value = (value.astype(F32) + local[b]).astype(BF16)
            prop[s, b // pieces, :, LANES * j : LANES * (j + 1)] = value


def total_over(parts):
    first = parts[0]
    for part in parts[1:]:
        first = first + part
    return first


def few_bands(features, aligned, cotangent, weight, src_tile, src_blk):
    frames, channels, height, columns = features.shape
    inner = channels + aligned.shape[1]
    tiles = lax.axis_size("tile")
    groups = lax.axis_size("tm")
    chips = tiles // 2
    tile = lax.axis_index("tile")
    group = lax.axis_index("tm")
    core = tile % 2
    pos = jnp.stack([core, tile // 2, group]).astype(jnp.int32)

    cores = [(i, i ^ 1) for i in range(tiles)]
    joints = [(2 * z + 1, 2 * z + 2) for z in range(chips - 1)]
    joints += [(b, a) for a, b in joints]

    def hop(k):
        route = []
        for z in range(k, chips - 1):
            route += [(2 * z, 2 * z + 2), (2 * (chips - 1 - z) + 1, 2 * (chips - 1 - z) - 1)]
        return route

    def to_tile(block, route):
        return lax.ppermute(block, "tile", route)

    def to_group(block, route):
        return lax.ppermute(block, "tm", route)

    pieces = columns // LANES
    u = jnp.transpose(jnp.concatenate((features, aligned), axis=1), (0, 2, 1, 3))
    u = after(u)
    rout = to_tile(lax.dynamic_index_in_dim(u, core, 1, keepdims=False), joints)
    rin = to_tile(lax.dynamic_index_in_dim(u, 1 - core, 1, keepdims=False), cores)
    cot = jnp.transpose(cotangent, (0, 2, 1, 3))
    w3 = weight.reshape(3, 3 * channels, inner)
    codes = (src_tile * 8 + src_blk).reshape(1, -1).astype(BF16)
    tab = jnp.pad(codes, ((0, TABLE_ROWS - 1), (0, LANES - codes.shape[1])))

    halo = pltpu.VMEM((2, frames, inner, columns), BF16)
    msg_rows = 2 * frames * pieces * channels + TABLE_ROWS
    msg, g3 = call(
        forward_kernel,
        [
            jax.ShapeDtypeStruct((msg_rows, LANES), BF16),
            jax.ShapeDtypeStruct((frames, 2, 3 * channels, columns), BF16),
        ],
        (pos, u, rin, rout, cot, w3, tab),
        1,
        [halo],
    )

    half_shapes = [jax.ShapeDtypeStruct((9 * channels // n, inner), F32) for n in (2, 4, 8)]
    weight_shapes = [
        jax.ShapeDtypeStruct((3 * n, 3 * channels), BF16) for n in (inner - channels, channels)
    ]
    swaps = [[(i, i ^ k) for i in range(groups)] for k in range(groups)]
    turns = [[(2 * z + c, 2 * (z ^ k) + c) for z in range(chips) for c in range(2)] for k in range(chips)]
    bands = 2 * chips
    sums_shape = (3, 2 * pieces, channels, LANES)
    work = [
        pltpu.VMEM((frames, 2 * bands + 2, channels, columns), BF16),
        pltpu.VMEM((bands, LANES), jnp.int32),
        pltpu.SMEM((bands, LANES), jnp.int32),
        pltpu.SMEM((4 * pieces * bands + 1,), jnp.int32),
        pltpu.VMEM((frames, 2 * bands, pieces, 2, channels, LANES), BF16),
        pltpu.SemaphoreType.DMA,
    ]

    other = to_tile(msg, cores)
    own = jnp.stack((msg, other))
    near1 = to_tile(own, hop(0))
    keep, send, wa, wf = call(
        taps_kernel,
        [half_shapes[0], half_shapes[0], *weight_shapes],
        (pos, u, rin, rout, after(g3, own), w3),
        1,
        [halo, pltpu.VMEM((9 * channels, inner), F32)],
    )
    got = to_tile(send, cores)
    part_rows = 9 * channels // (2 * groups)
    part_shape = jax.ShapeDtypeStruct((part_rows, inner), F32)
    shares = call(shares_kernel, [part_shape] * groups, (pos, keep, got), 1, micros=0.6)
    share = total_over([shares[0]] + [to_group(shares[k], swaps[k]) for k in range(1, groups)])
    near2 = to_tile(near1, hop(1))
    far1 = to_tile(near1, cores)
    share = after(share, far1)
    sums, feat = call(
        lambda *refs: stage_kernel(1, chips, *refs),
        [
            jax.ShapeDtypeStruct(sums_shape, F32),
            jax.ShapeDtypeStruct((frames, 2, channels, columns), BF16),
        ],
        (pos, own, near1, far1, wa, wf),
        1,
        work,
        micros=6.0,
    )
    share = total_over([share] + [to_tile(share, turns[k]) for k in range(1, chips)])
    pixels = frames * groups * height * tiles * columns
    share = share * (1.0 / math.sqrt(pixels))
    near3 = to_tile(near2, hop(2))
    far2 = to_tile(near2, cores)
    (sums,) = call(
        lambda *refs: stage_kernel(2, chips, *refs),
        [jax.ShapeDtypeStruct(sums_shape, F32)],
        (pos, near1, far1, near2, far2, wa, sums),
        1,
        work,
        micros=4.0,
    )
    share = after(share, far2)
    mine = jnp.stack([share] + [to_group(share, swaps[k]) for k in range(1, groups)])
    near3 = after(near3, mine, sums)
    far3 = to_tile(near3, cores)
    passed, local = call(
        lambda *refs: final_stage_kernel(3, chips, *refs),
        [jax.ShapeDtypeStruct((2, *sums_shape[1:]), BF16), jax.ShapeDtypeStruct(sums_shape[1:], F32)],
        (pos, near2, far2, near3, far3, wa, sums),
        1,
        [pltpu.VMEM(sums_shape, F32)] + work,
        micros=4.0,
    )
    passed = to_group(passed, [(m + 1, m) for m in range(groups - 1)])
    theirs = to_tile(mine, cores)
    (grad_weight,) = call(
        assemble_kernel, [jax.ShapeDtypeStruct((9 * channels, inner), F32)], (pos, mine, theirs), 1
    )

    (prop,) = call(
        last_kernel, [jax.ShapeDtypeStruct((2, 2, channels, columns), BF16)], (passed, local), 0
    )
    return (
        grad_weight.reshape(9, channels, inner),
        jnp.transpose(feat, (0, 2, 1, 3)),
        jnp.transpose(prop, (0, 2, 1, 3)),
    )


def with_halo(cells, sides, width):
    for axis, dim in sides:
        count = lax.axis_size(axis)
        ends = count - 1
        head = lax.slice_in_dim(cells, 0, width, axis=dim)
        tail = lax.slice_in_dim(cells, cells.shape[dim] - width, cells.shape[dim], axis=dim)
        cells = jnp.concatenate(
            [
                lax.ppermute(tail, axis, [(i, (i + 1) % count) for i in range(ends)]),
                cells,
                lax.ppermute(head, axis, [((i + 1) % count, i) for i in range(ends)]),
            ],
            axis=dim,
        )
    return cells


def passed_along(block, axis, distance):
    devices = range(lax.axis_size(axis))
    route = [(i - distance, i) for i in devices if i - distance in devices]
    return lax.ppermute(block, axis, route)


def pad_columns(values):
    return jnp.pad(values, ((0, 0), (0, 0), (0, 0), (1, 1)))


def conv_forward(weight, padded_input, height):
    columns = padded_input.shape[3] - 2
    summed = jnp.zeros((padded_input.shape[0], weight.shape[1], height, columns), jnp.float32)
    for row_tap in range(3):
        for col_tap in range(3):
            window = padded_input[:, :, row_tap : row_tap + height, col_tap : col_tap + columns]
            summed = summed + jnp.einsum(
                "oi,firc->forc",
                weight[3 * row_tap + col_tap],
                window,
                preferred_element_type=jnp.float32,
            )
    return summed


def conv_transpose(weight, padded_input, height):
    columns = padded_input.shape[3] - 2
    summed = jnp.zeros((padded_input.shape[0], weight.shape[2], height, columns), jnp.float32)
    for row_tap in range(3):
        for col_tap in range(3):
            window = padded_input[
                :, :, 2 - row_tap : 2 - row_tap + height, 2 - col_tap : 2 - col_tap + columns
            ]
            summed = summed + jnp.einsum(
                "oi,forc->firc",
                weight[3 * row_tap + col_tap],
                window,
                preferred_element_type=jnp.float32,
            )
    return summed.astype(jnp.bfloat16)


def weight_grad(padded_input, cot_pre):
    height = cot_pre.shape[2]
    columns = cot_pre.shape[3]
    term_list = []
    for row_tap in range(3):
        for col_tap in range(3):
            window = padded_input[:, :, row_tap : row_tap + height, col_tap : col_tap + columns]
            term_list.append(
                jnp.einsum("forc,firc->oi", cot_pre, window, preferred_element_type=jnp.float32)
            )
    return jnp.stack(term_list)


def build_slots(aligned_grad, tiles, blocks, tile_count, capacity):
    frames, stacked, height, columns = aligned_grad.shape
    block_count = tiles.shape[1]
    pixels = height * columns // block_count
    pieces = aligned_grad.reshape(frames, 2, stacked // 2, block_count, pixels)
    row_ids = jnp.arange(2 * block_count, dtype=jnp.int32)
    destination = jnp.swapaxes(tiles, 1, 2).reshape(frames, 2 * block_count)
    target_code = (
        jnp.swapaxes(blocks, 1, 2).reshape(frames, 2 * block_count)
        + (row_ids // block_count * block_count)[None, :]
    )
    tile_hit_count = (
        destination[:, :, None] == jnp.arange(tile_count, dtype=jnp.int32)[None, None, :]
    ).astype(jnp.int32)
    earlier = jnp.cumsum(tile_hit_count, axis=1) - tile_hit_count
    slot_ids = destination * capacity + jnp.sum(tile_hit_count * earlier, axis=2)
    source_selector = (
        slot_ids[:, None, :] == jnp.arange(tile_count * capacity, dtype=jnp.int32)[None, :, None]
    ).astype(jnp.bfloat16)
    target_onehot = (target_code[:, :, None] == row_ids[None, None, :]).astype(jnp.bfloat16)
    placing = jnp.einsum(
        "anu,auo->ano", source_selector, target_onehot, preferred_element_type=jnp.float32
    ).astype(jnp.bfloat16)
    select_split = source_selector.reshape(frames, tile_count * capacity, 2, block_count)
    payload = jnp.einsum(
        "fsob,focbp->fscp", select_split, pieces, preferred_element_type=jnp.float32
    ).astype(jnp.bfloat16)
    return (payload, placing)


def place_blocks(received):
    payload, placing = received
    return jnp.einsum("fsb,fscp->fcbp", placing, payload, preferred_element_type=jnp.float32)


def deliver(aligned_grad, tiles, blocks, tile_count, capacity):
    payload, placing = build_slots(aligned_grad, tiles, blocks, tile_count, capacity)
    return place_blocks(
        (
            lax.all_to_all(payload, "tile", split_axis=1, concat_axis=1, tiled=True),
            lax.all_to_all(placing, "tile", split_axis=1, concat_axis=1, tiled=True),
        )
    )


def many_bands(features, aligned, cotangent, weight, src_tile, src_blk):
    frames, channels, height, columns = features.shape
    inputs = jnp.concatenate((features, aligned), axis=1)
    padded_in = pad_columns(with_halo(inputs, (("tile", 2),), 1))
    preact = conv_forward(weight, padded_in, height)
    cot_pre = (cotangent * act_slope(preact)).astype(jnp.bfloat16)
    padded_cot = pad_columns(with_halo(cot_pre, (("tile", 2),), 1))
    tile_count = lax.axis_size("tile")
    block_count = src_tile.shape[1]
    capacity = max(2, (4 * block_count + tile_count - 1) // tile_count)
    input_grad = conv_transpose(weight, padded_cot, height)
    local_weight = weight_grad(padded_in, cot_pre)
    feat_grad = input_grad[:, :channels]
    aligned_grad = input_grad[:, channels:]
    arrived = deliver(aligned_grad, src_tile, src_blk, tile_count, capacity)
    landed = arrived.reshape(frames, channels, 2, height, columns)
    extended = jnp.pad(landed[:, :, 0], ((1, 1), (0, 0), (0, 0), (0, 0))) + jnp.pad(
        landed[:, :, 1], ((0, 2), (0, 0), (0, 0), (0, 0))
    )
    arriving = passed_along(extended[:2], "tm", -1)
    resident = extended[2:]
    resident = jnp.concatenate((resident[: frames - 2], resident + arriving), axis=0)
    total_weight = lax.psum(local_weight, ("tm", "tile"))
    pixels = frames * lax.axis_size("tm") * height * tile_count * columns
    grad_weight = total_weight * (1.0 / math.sqrt(pixels))
    return (grad_weight, feat_grad, resident.astype(jnp.bfloat16))


def solution(mesh):
    in_specs = (
        P("tm", None, "tile", None),
        P("tm", None, "tile", None),
        P("tm", None, "tile", None),
        P(),
        P("tm", "tile", None),
        P("tm", "tile", None),
    )
    out_specs = (P(), P("tm", None, "tile", None), P("tm", None, "tile", None))
    few = mesh.shape["tile"] == 8 and mesh.shape["tm"] == 4
    body = few_bands if few else many_bands
    return jax.shard_map(body, mesh=mesh, in_specs=in_specs, out_specs=out_specs, check_vma=False)
```

```python
import math

import jax
import jax.numpy as jnp
from jax import lax
from jax.experimental import pallas as pl
from jax.experimental.pallas import tpu as pltpu
from jax.sharding import PartitionSpec as P

F32 = jnp.float32
BF16 = jnp.bfloat16


def act_slope(preact):
    return 0.1 + 0.9 * jax.nn.sigmoid(preact)


TABLE_ROWS = 16
LANES = 128


def full(memory_space=pltpu.VMEM):
    return pl.BlockSpec(memory_space=memory_space)


def call(kernel, out_shapes, args, scalars, scratch=(), micros=0.0):
    specs = [full(pltpu.SMEM)] * scalars + [full()] * (len(args) - scalars)
    return pl.pallas_call(
        kernel,
        out_shape=out_shapes,
        in_specs=specs,
        out_specs=[full()] * len(out_shapes),
        scratch_shapes=list(scratch),
        cost_estimate=pl.CostEstimate(flops=int(micros * 1e9), bytes_accessed=0, transcendentals=0),
        compiler_params=pltpu.CompilerParams(vmem_limit_bytes=24 << 20),
    )(*args)


def after(value, *others):
    return lax.optimization_barrier((value, *others))[0]


def from_left(values):
    lane = lax.broadcasted_iota(jnp.int32, values.shape, 1)
    return jnp.where(lane == 0, 0.0, pltpu.roll(values, 1, 1))


def from_right(values):
    columns = values.shape[1]
    lane = lax.broadcasted_iota(jnp.int32, values.shape, 1)
    return jnp.where(lane == columns - 1, 0.0, pltpu.roll(values, columns - 1, 1))


def taps_of(row):
    wide = row.astype(F32)
    return (from_right(wide).astype(BF16), row, from_left(wide).astype(BF16))


def forward_kernel(pos, u, rin, rout, cot, w3, tab, msg, g3, halo):
    core = pos[0]
    frames, _, ch, columns = cot.shape
    pieces = columns // LANES
    halo[core] = rout[...]
    halo[1 - core] = rin[...]
    for f in range(frames):
        rows = (halo.at[0, f], u.at[f, 0], u.at[f, 1], halo.at[1, f])
        for r in range(2):
            taps = jnp.dot(w3[0], rows[r][...], preferred_element_type=F32)
            taps += jnp.dot(w3[1], rows[r + 1][...], preferred_element_type=F32)
            taps += jnp.dot(w3[2], rows[r + 2][...], preferred_element_type=F32)
            z = taps[ch : 2 * ch] + from_left(taps[:ch]) + from_right(taps[2 * ch :])
            g = (cot[f, r].astype(F32) * act_slope(z)).astype(BF16)
            for j in range(pieces):
                at = ((2 * f + r) * pieces + j) * ch
                msg[at : at + ch] = g[:, LANES * j : LANES * (j + 1)]
            for k, part in enumerate(taps_of(g)):
                g3[f, r, k * ch : (k + 1) * ch] = part
    msg[2 * frames * pieces * ch :] = tab[...]


def taps_kernel(pos, u, rin, rout, g3, w3, keep, send, wa, wf, halo, total):
    core = pos[0]
    size = g3.shape[2]
    half = keep.shape[0]
    halo[core] = rout[...]
    halo[1 - core] = rin[...]
    for ky in range(3):
        acc = jnp.zeros((size, u.shape[2]), F32)
        for f in range(u.shape[0]):
            rows = (halo.at[0, f], u.at[f, 0], u.at[f, 1], halo.at[1, f])
            for r in range(2):
                acc += lax.dot_general(
                    g3[f, r], rows[r + ky][...], (((1,), (1,)), ((), ())), preferred_element_type=F32
                )
        total[ky * size : (ky + 1) * size] = acc
    keep[...] = total[pl.ds(pl.multiple_of(core * half, 8), half)]
    send[...] = total[pl.ds(pl.multiple_of((1 - core) * half, 8), half)]
    ch = size // 3
    for kx in range(3):
        rows = [w3[ky, kx * ch : (kx + 1) * ch] for ky in (2, 1, 0)]
        turned = jnp.transpose(jnp.concatenate(rows, axis=0).astype(F32)).astype(BF16)
        wf[kx * ch : (kx + 1) * ch] = turned[:ch]
        wa[2 * kx * ch : 2 * (kx + 1) * ch] = turned[ch:]


def shares_kernel(pos, keep, got, own, *others):
    group = pos[2]
    part = own.shape[0]
    for k, out in enumerate((own, *others)):
        at = pl.ds(pl.multiple_of((group ^ k) * part, 8), part)
        out[...] = keep[at] + got[at]


def assemble_kernel(pos, mine, theirs, out):
    core, group = pos[0], pos[2]
    part = mine.shape[1]
    parts = mine.shape[0]
    for source, side in ((mine, core), (theirs, 1 - core)):
        for k in range(parts):
            at = (side * parts + (group ^ k)) * part
            out[pl.ds(pl.multiple_of(at, 8), part)] = source[k]


def collect_codes(entries, chips, tabs):
    for ref, where, first in entries:

        @pl.when((where >= 0) & (where < chips))
        def _(ref=ref, where=where, first=first):
            for h in range(2):
                band = 2 * where + (first if h == 0 else 1 - first)
                codes = ref[h, ref.shape[1] - TABLE_ROWS :].astype(F32).astype(jnp.int32)
                tabs[pl.ds(band, 1)] = codes[:1]


def collect(entries, chips, g):
    frames, _, ch, columns = g.shape
    pieces = columns // LANES
    for ref, where, first in entries:

        @pl.when((where >= 0) & (where < chips))
        def _(ref=ref, where=where, first=first):
            for h in range(2):
                band = 2 * where + (first if h == 0 else 1 - first)
                for f in range(frames):
                    for r in range(2):
                        for j in range(pieces):
                            at = ((2 * f + r) * pieces + j) * ch
                            lanes = slice(LANES * j, LANES * (j + 1))
                            g[f, 2 * band + r + 1, :, lanes] = ref[h, at : at + ch]


def convolved(weights, window):
    taps = jnp.dot(weights[...], window, preferred_element_type=F32)
    size = taps.shape[0] // 3
    total = taps[size : 2 * size] + from_right(taps[:size]) + from_left(taps[2 * size :])
    return total.astype(BF16)


def spread(count_rows, row_at, me, g, weights, codes, hits, gu, sums):
    frames, rows, ch, columns = g.shape
    pieces = columns // LANES

    def two_rows(p, count):
        for i in range(2):
            known = 2 * p + i < count_rows
            r = jnp.minimum(row_at(2 * p + i), rows - 3)
            for f in range(frames):
                value = convolved(weights, g[f, pl.ds(r, 3)].reshape(3 * ch, columns))
                for j in range(pieces):
                    for q in range(2):
                        gu[f, r, j, q] = value[q * ch : (q + 1) * ch, LANES * j : LANES * (j + 1)]
                for k in range(2 * pieces):
                    lane = (2 * f + r % 2) * (2 * pieces) + k
                    hits[count] = (r // 2) * LANES + lane
                    named = lax.shift_right_logical(codes[r // 2, lane], 3) == me
                    count += (known & named).astype(jnp.int32)
        return count

    count = lax.fori_loop(0, (count_rows + 1) // 2, two_rows, 0)

    def one_hit(k, _):
        hit = hits[k]
        band, lane = hit // LANES, hit % LANES
        f, block, q = lane // (4 * pieces), (lane % (4 * pieces)) // 2, lane % 2
        target = codes[band, lane] % 8
        sums[f + 1 - q, target] += gu[f, 2 * band + block // pieces, block % pieces, q].astype(F32)
        return 0

    lax.fori_loop(0, count, one_hit, 0)


def ready_rows(chip, reach, chips):
    low, high = jnp.maximum(chip - reach, 0), jnp.minimum(chip + reach, chips - 1)
    return 4 * low + (low > 0).astype(jnp.int32), 4 * high + 4 - (high < chips - 1).astype(jnp.int32)


def side(ref, reach, pos, away):
    core, chip = pos[0], pos[1]
    step = (1 - 2 * core) * reach
    return (ref, chip + step, 1 - core) if away else (ref, chip - step, core)


def stage(old, reach, chips, entries, pos, weights, sums, g, tabs, codes, hits, gu, sem):
    core, chip = pos[0], pos[1]
    me = 2 * chip + core
    collect_codes(entries, chips, tabs)
    copy = pltpu.make_async_copy(tabs, codes, sem)
    copy.start()
    frames, rows, ch, columns = g.shape
    zero = jnp.zeros((ch, columns), BF16)
    for f in range(frames):
        g[f, 0] = zero
        g[f, rows - 1] = zero
    collect(entries, chips, g)
    copy.wait()
    low, high = ready_rows(chip, reach, chips)
    if old is None:
        spread(high - low, lambda i: low + i, me, g, weights, codes, hits, gu, sums)
    else:
        old_low, old_high = ready_rows(chip, old, chips)
        below = old_low - low
        spread(
            below + high - old_high,
            lambda i: jnp.where(i < below, low + i, old_high + i - below),
            me, g, weights, codes, hits, gu, sums,
        )


def first_stage_kernel(chips, pos, own, wa, sums, *work):
    sums[...] = jnp.zeros(sums.shape, F32)
    stage(None, 0, chips, [side(own, 0, pos, False)], pos, wa, sums, *work)


def middle_stage_kernel(chips, pos, own, near1, near2, far, wa, sums_in, sums, *work):
    sums[...] = sums_in[...]
    entries = [side(own, 0, pos, False), side(near1, 1, pos, False), side(near2, 2, pos, False)]
    entries += [side(far.at[0], 1, pos, True), side(far.at[1], 2, pos, True)]
    stage(0, 2, chips, entries, pos, wa, sums, *work)


def final_stage_kernel(chips, pos, near2, far, near3, far3, wa, sums_in, passed, local, sums, *work):
    sums[...] = sums_in[...]
    entries = [side(near2, 2, pos, False), side(far.at[1], 2, pos, True)]
    entries += [side(near3, 3, pos, False), side(far3, 3, pos, True)]
    stage(2, 3, chips, entries, pos, wa, sums, *work)
    for s in range(2):
        passed[s] = sums[s].astype(BF16)
    local[...] = sums[2]


def features_kernel(pos, own, near, wf, feat, rows4):
    core = pos[0]
    frames, _, ch, columns = feat.shape
    pieces = columns // LANES
    for f in range(frames):
        for j in range(pieces):
            lanes = slice(LANES * j, LANES * (j + 1))

            def at(r):
                return pl.ds(pl.multiple_of(((2 * f + r) * pieces + j) * ch, ch), ch)

            rows4[3 * core, :, lanes] = near[1, at(1 - core)]
            rows4[3 * (1 - core), :, lanes] = own[1, at(core)]
            for r in range(2):
                rows4[1 + r, :, lanes] = own[0, at(r)]
        for r in range(2):
            feat[f, r] = convolved(wf, rows4[r : r + 3].reshape(3 * ch, columns))


def last_kernel(passed, local, prop):
    ch = local.shape[1]
    pieces = prop.shape[3] // LANES
    for s in range(2):
        for b in range(2 * pieces):
            j = b % pieces
            value = passed[s, b]
            if s == 0:
                value = (value.astype(F32) + local[b]).astype(BF16)
            prop[s, b // pieces, :, LANES * j : LANES * (j + 1)] = value


def total_over(parts):
    first = parts[0]
    for part in parts[1:]:
        first = first + part
    return first


def few_bands(features, aligned, cotangent, weight, src_tile, src_blk):
    frames, channels, height, columns = features.shape
    inner = channels + aligned.shape[1]
    tiles = lax.axis_size("tile")
    groups = lax.axis_size("tm")
    chips = tiles // 2
    tile = lax.axis_index("tile")
    group = lax.axis_index("tm")
    core = tile % 2
    pos = jnp.stack([core, tile // 2, group]).astype(jnp.int32)

    cores = [(i, i ^ 1) for i in range(tiles)]
    joints = [(2 * z + 1, 2 * z + 2) for z in range(chips - 1)]
    joints += [(b, a) for a, b in joints]

    def hop(k):
        route = []
        for z in range(k, chips - 1):
            route += [(2 * z, 2 * z + 2), (2 * (chips - 1 - z) + 1, 2 * (chips - 1 - z) - 1)]
        return route

    def to_tile(block, route):
        return lax.ppermute(block, "tile", route)

    def to_group(block, route):
        return lax.ppermute(block, "tm", route)

    pieces = columns // LANES
    u = jnp.transpose(jnp.concatenate((features, aligned), axis=1), (0, 2, 1, 3))
    u = after(u)
    rout = to_tile(lax.dynamic_index_in_dim(u, core, 1, keepdims=False), joints)
    rin = to_tile(lax.dynamic_index_in_dim(u, 1 - core, 1, keepdims=False), cores)
    cot = jnp.transpose(cotangent, (0, 2, 1, 3))
    w3 = weight.reshape(3, 3 * channels, inner)
    codes = (src_tile * 8 + src_blk).reshape(1, -1).astype(BF16)
    tab = jnp.pad(codes, ((0, TABLE_ROWS - 1), (0, LANES - codes.shape[1])))

    halo = pltpu.VMEM((2, frames, inner, columns), BF16)
    msg_rows = 2 * frames * pieces * channels + TABLE_ROWS
    msg, g3 = call(
        forward_kernel,
        [
            jax.ShapeDtypeStruct((msg_rows, LANES), BF16),
            jax.ShapeDtypeStruct((frames, 2, 3 * channels, columns), BF16),
        ],
        (pos, u, rin, rout, cot, w3, tab),
        1,
        [halo],
    )

    half_shape = jax.ShapeDtypeStruct((9 * channels // 2, inner), F32)
    weight_shapes = [
        jax.ShapeDtypeStruct((3 * n, 3 * channels), BF16) for n in (inner - channels, channels)
    ]
    swaps = [[(i, i ^ k) for i in range(groups)] for k in range(groups)]
    turns = [[(2 * z + c, 2 * (z ^ k) + c) for z in range(chips) for c in range(2)] for k in range(chips)]
    bands = 2 * chips
    sums_shape = (3, 2 * pieces, channels, LANES)
    work = [
        pltpu.VMEM((frames, 2 * bands + 2, channels, columns), BF16),
        pltpu.VMEM((bands, LANES), jnp.int32),
        pltpu.SMEM((bands, LANES), jnp.int32),
        pltpu.SMEM((4 * pieces * bands + 1,), jnp.int32),
        pltpu.VMEM((frames, 2 * bands, pieces, 2, channels, LANES), BF16),
        pltpu.SemaphoreType.DMA,
    ]

    other = to_tile(msg, cores)
    own = jnp.stack((msg, other))
    near1 = to_tile(own, hop(0))
    keep, send, wa, wf = call(
        taps_kernel,
        [half_shape, half_shape, *weight_shapes],
        (pos, u, rin, rout, after(g3, own), w3),
        1,
        [halo, pltpu.VMEM((9 * channels, inner), F32)],
        micros=0.0,
    )
    got = to_tile(send, cores)
    part_rows = 9 * channels // (2 * groups)
    part_shape = jax.ShapeDtypeStruct((part_rows, inner), F32)
    shares = call(shares_kernel, [part_shape] * groups, (pos, keep, got), 1, micros=0.0)

    (sums,) = call(
        lambda *refs: first_stage_kernel(chips, *refs),
        [jax.ShapeDtypeStruct(sums_shape, F32)],
        (pos, own, wa),
        1,
        work,
        micros=0.0,
    )
    near1 = after(near1, sums, *shares)
    near2 = to_tile(near1, hop(1))
    share = total_over([shares[0]] + [to_group(shares[k], swaps[k]) for k in range(1, groups)])
    pixels = frames * groups * height * tiles * columns
    near2 = after(near2, share)
    near3 = to_tile(near2, hop(2))
    far = to_tile(jnp.stack((near1, near2)), cores)
    share = after(share, far)
    share = total_over([share] + [to_tile(share, turns[k]) for k in range(1, chips)])
    share = share * (1.0 / math.sqrt(pixels))
    (sums,) = call(
        lambda *refs: middle_stage_kernel(chips, *refs),
        [jax.ShapeDtypeStruct(sums_shape, F32)],
        (pos, own, near1, near2, far, wa, sums),
        1,
        work,
        micros=2.0,
    )
    share = after(share, sums)
    near3 = after(near3, share, sums)
    far3 = to_tile(near3, cores)
    passed, local = call(
        lambda *refs: final_stage_kernel(chips, *refs),
        [jax.ShapeDtypeStruct((2, *sums_shape[1:]), BF16), jax.ShapeDtypeStruct(sums_shape[1:], F32)],
        (pos, near2, far, near3, far3, wa, sums),
        1,
        [pltpu.VMEM(sums_shape, F32)] + work,
        micros=0.0,
    )
    mine = jnp.stack([share] + [to_group(share, swaps[k]) for k in range(1, groups)])
    (feat,) = call(
        features_kernel,
        [jax.ShapeDtypeStruct((frames, 2, channels, columns), BF16)],
        (pos, after(own, passed), near1, wf),
        1,
        [pltpu.VMEM((4, channels, columns), BF16)],
    )
    passed = to_group(passed, [(m + 1, m) for m in range(groups - 1)])
    theirs = to_tile(mine, cores)
    (grad_weight,) = call(
        assemble_kernel, [jax.ShapeDtypeStruct((9 * channels, inner), F32)], (pos, mine, theirs), 1
    )

    (prop,) = call(
        last_kernel, [jax.ShapeDtypeStruct((2, 2, channels, columns), BF16)], (passed, local), 0
    )
    return (
        grad_weight.reshape(9, channels, inner),
        jnp.transpose(feat, (0, 2, 1, 3)),
        jnp.transpose(prop, (0, 2, 1, 3)),
    )


def with_halo(cells, sides, width):
    for axis, dim in sides:
        count = lax.axis_size(axis)
        ends = count - 1
        head = lax.slice_in_dim(cells, 0, width, axis=dim)
        tail = lax.slice_in_dim(cells, cells.shape[dim] - width, cells.shape[dim], axis=dim)
        cells = jnp.concatenate(
            [
                lax.ppermute(tail, axis, [(i, (i + 1) % count) for i in range(ends)]),
                cells,
                lax.ppermute(head, axis, [((i + 1) % count, i) for i in range(ends)]),
            ],
            axis=dim,
        )
    return cells


def passed_along(block, axis, distance):
    devices = range(lax.axis_size(axis))
    route = [(i - distance, i) for i in devices if i - distance in devices]
    return lax.ppermute(block, axis, route)


def pad_columns(values):
    return jnp.pad(values, ((0, 0), (0, 0), (0, 0), (1, 1)))


def conv_forward(weight, padded_input, height):
    columns = padded_input.shape[3] - 2
    summed = jnp.zeros((padded_input.shape[0], weight.shape[1], height, columns), jnp.float32)
    for row_tap in range(3):
        for col_tap in range(3):
            window = padded_input[:, :, row_tap : row_tap + height, col_tap : col_tap + columns]
            summed = summed + jnp.einsum(
                "oi,firc->forc",
                weight[3 * row_tap + col_tap],
                window,
                preferred_element_type=jnp.float32,
            )
    return summed


def conv_transpose(weight, padded_input, height):
    columns = padded_input.shape[3] - 2
    summed = jnp.zeros((padded_input.shape[0], weight.shape[2], height, columns), jnp.float32)
    for row_tap in range(3):
        for col_tap in range(3):
            window = padded_input[
                :, :, 2 - row_tap : 2 - row_tap + height, 2 - col_tap : 2 - col_tap + columns
            ]
            summed = summed + jnp.einsum(
                "oi,forc->firc",
                weight[3 * row_tap + col_tap],
                window,
                preferred_element_type=jnp.float32,
            )
    return summed.astype(jnp.bfloat16)


def weight_grad(padded_input, cot_pre):
    height = cot_pre.shape[2]
    columns = cot_pre.shape[3]
    term_list = []
    for row_tap in range(3):
        for col_tap in range(3):
            window = padded_input[:, :, row_tap : row_tap + height, col_tap : col_tap + columns]
            term_list.append(
                jnp.einsum("forc,firc->oi", cot_pre, window, preferred_element_type=jnp.float32)
            )
    return jnp.stack(term_list)


def build_slots(aligned_grad, tiles, blocks, tile_count, capacity):
    frames, stacked, height, columns = aligned_grad.shape
    block_count = tiles.shape[1]
    pixels = height * columns // block_count
    pieces = aligned_grad.reshape(frames, 2, stacked // 2, block_count, pixels)
    row_ids = jnp.arange(2 * block_count, dtype=jnp.int32)
    destination = jnp.swapaxes(tiles, 1, 2).reshape(frames, 2 * block_count)
    target_code = (
        jnp.swapaxes(blocks, 1, 2).reshape(frames, 2 * block_count)
        + (row_ids // block_count * block_count)[None, :]
    )
    tile_hit_count = (
        destination[:, :, None] == jnp.arange(tile_count, dtype=jnp.int32)[None, None, :]
    ).astype(jnp.int32)
    earlier = jnp.cumsum(tile_hit_count, axis=1) - tile_hit_count
    slot_ids = destination * capacity + jnp.sum(tile_hit_count * earlier, axis=2)
    source_selector = (
        slot_ids[:, None, :] == jnp.arange(tile_count * capacity, dtype=jnp.int32)[None, :, None]
    ).astype(jnp.bfloat16)
    target_onehot = (target_code[:, :, None] == row_ids[None, None, :]).astype(jnp.bfloat16)
    placing = jnp.einsum(
        "anu,auo->ano", source_selector, target_onehot, preferred_element_type=jnp.float32
    ).astype(jnp.bfloat16)
    select_split = source_selector.reshape(frames, tile_count * capacity, 2, block_count)
    payload = jnp.einsum(
        "fsob,focbp->fscp", select_split, pieces, preferred_element_type=jnp.float32
    ).astype(jnp.bfloat16)
    return (payload, placing)


def place_blocks(received):
    payload, placing = received
    return jnp.einsum("fsb,fscp->fcbp", placing, payload, preferred_element_type=jnp.float32)


def deliver(aligned_grad, tiles, blocks, tile_count, capacity):
    payload, placing = build_slots(aligned_grad, tiles, blocks, tile_count, capacity)
    return place_blocks(
        (
            lax.all_to_all(payload, "tile", split_axis=1, concat_axis=1, tiled=True),
            lax.all_to_all(placing, "tile", split_axis=1, concat_axis=1, tiled=True),
        )
    )


def many_bands(features, aligned, cotangent, weight, src_tile, src_blk):
    frames, channels, height, columns = features.shape
    inputs = jnp.concatenate((features, aligned), axis=1)
    padded_in = pad_columns(with_halo(inputs, (("tile", 2),), 1))
    preact = conv_forward(weight, padded_in, height)
    cot_pre = (cotangent * act_slope(preact)).astype(jnp.bfloat16)
    padded_cot = pad_columns(with_halo(cot_pre, (("tile", 2),), 1))
    tile_count = lax.axis_size("tile")
    block_count = src_tile.shape[1]
    capacity = max(2, (4 * block_count + tile_count - 1) // tile_count)
    input_grad = conv_transpose(weight, padded_cot, height)
    local_weight = weight_grad(padded_in, cot_pre)
    feat_grad = input_grad[:, :channels]
    aligned_grad = input_grad[:, channels:]
    arrived = deliver(aligned_grad, src_tile, src_blk, tile_count, capacity)
    landed = arrived.reshape(frames, channels, 2, height, columns)
    extended = jnp.pad(landed[:, :, 0], ((1, 1), (0, 0), (0, 0), (0, 0))) + jnp.pad(
        landed[:, :, 1], ((0, 2), (0, 0), (0, 0), (0, 0))
    )
    arriving = passed_along(extended[:2], "tm", -1)
    resident = extended[2:]
    resident = jnp.concatenate((resident[: frames - 2], resident + arriving), axis=0)
    total_weight = lax.psum(local_weight, ("tm", "tile"))
    pixels = frames * lax.axis_size("tm") * height * tile_count * columns
    grad_weight = total_weight * (1.0 / math.sqrt(pixels))
    return (grad_weight, feat_grad, resident.astype(jnp.bfloat16))


def solution(mesh):
    in_specs = (
        P("tm", None, "tile", None),
        P("tm", None, "tile", None),
        P("tm", None, "tile", None),
        P(),
        P("tm", "tile", None),
        P("tm", "tile", None),
    )
    out_specs = (P(), P("tm", None, "tile", None), P("tm", None, "tile", None))
    few = mesh.shape["tile"] == 8 and mesh.shape["tm"] == 4
    body = few_bands if few else many_bands
    return jax.shard_map(body, mesh=mesh, in_specs=in_specs, out_specs=out_specs, check_vma=False)
```

```python
import math

import jax
import jax.numpy as jnp
from jax import lax
from jax.experimental import pallas as pl
from jax.experimental.pallas import tpu as pltpu
from jax.sharding import PartitionSpec as P

F32 = jnp.float32
BF16 = jnp.bfloat16


def act_slope(preact):
    return 0.1 + 0.9 * jax.nn.sigmoid(preact)


TABLE_ROWS = 16
LANES = 128


def full(memory_space=pltpu.VMEM):
    return pl.BlockSpec(memory_space=memory_space)


def call(kernel, out_shapes, args, scalars, scratch=(), micros=0.0):
    specs = [full(pltpu.SMEM)] * scalars + [full()] * (len(args) - scalars)
    return pl.pallas_call(
        kernel,
        out_shape=out_shapes,
        in_specs=specs,
        out_specs=[full()] * len(out_shapes),
        scratch_shapes=list(scratch),
        cost_estimate=pl.CostEstimate(flops=int(micros * 1e9), bytes_accessed=0, transcendentals=0),
        compiler_params=pltpu.CompilerParams(vmem_limit_bytes=24 << 20),
    )(*args)


def after(value, *others):
    return lax.optimization_barrier((value, *others))[0]


def from_left(values):
    lane = lax.broadcasted_iota(jnp.int32, values.shape, 1)
    return jnp.where(lane == 0, 0.0, pltpu.roll(values, 1, 1))


def from_right(values):
    columns = values.shape[1]
    lane = lax.broadcasted_iota(jnp.int32, values.shape, 1)
    return jnp.where(lane == columns - 1, 0.0, pltpu.roll(values, columns - 1, 1))


def taps_of(row):
    wide = row.astype(F32)
    return (from_right(wide).astype(BF16), row, from_left(wide).astype(BF16))


def forward_kernel(pos, u, rin, rout, cot, w3, tab, msg, halo):
    core = pos[0]
    frames, _, ch, columns = cot.shape
    pieces = columns // LANES
    halo[core] = rout[...]
    halo[1 - core] = rin[...]
    for f in range(frames):
        rows = (halo.at[0, f], u.at[f, 0], u.at[f, 1], halo.at[1, f])
        for r in range(2):
            taps = jnp.dot(w3[0], rows[r][...], preferred_element_type=F32)
            taps += jnp.dot(w3[1], rows[r + 1][...], preferred_element_type=F32)
            taps += jnp.dot(w3[2], rows[r + 2][...], preferred_element_type=F32)
            z = taps[ch : 2 * ch] + from_left(taps[:ch]) + from_right(taps[2 * ch :])
            g = (cot[f, r].astype(F32) * act_slope(z)).astype(BF16)
            for j in range(pieces):
                at = ((2 * f + r) * pieces + j) * ch
                msg[at : at + ch] = g[:, LANES * j : LANES * (j + 1)]
    msg[2 * frames * pieces * ch :] = tab[...]


def taps_kernel(pos, u, rin, rout, msg, w3, keep, send, wa, wf, halo, total, g3):
    core = pos[0]
    frames, _, size, columns = g3.shape
    ch = size // 3
    pieces = columns // LANES
    half = keep.shape[0]
    halo[core] = rout[...]
    halo[1 - core] = rin[...]
    for f in range(frames):
        for r in range(2):
            at = (2 * f + r) * pieces * ch
            row = jnp.concatenate([msg[at + j * ch : at + (j + 1) * ch] for j in range(pieces)], axis=1)
            for k, part in enumerate(taps_of(row)):
                g3[f, r, k * ch : (k + 1) * ch] = part
    for ky in range(3):
        acc = jnp.zeros((size, u.shape[2]), F32)
        for f in range(u.shape[0]):
            rows = (halo.at[0, f], u.at[f, 0], u.at[f, 1], halo.at[1, f])
            for r in range(2):
                acc += lax.dot_general(
                    g3[f, r], rows[r + ky][...], (((1,), (1,)), ((), ())), preferred_element_type=F32
                )
        total[ky * size : (ky + 1) * size] = acc
    keep[...] = total[pl.ds(pl.multiple_of(core * half, 8), half)]
    send[...] = total[pl.ds(pl.multiple_of((1 - core) * half, 8), half)]
    for kx in range(3):
        rows = [w3[ky, kx * ch : (kx + 1) * ch] for ky in (2, 1, 0)]
        turned = jnp.transpose(jnp.concatenate(rows, axis=0).astype(F32)).astype(BF16)
        wf[kx * ch : (kx + 1) * ch] = turned[:ch]
        wa[2 * kx * ch : 2 * (kx + 1) * ch] = turned[ch:]


def shares_kernel(pos, keep, got, own, *others):
    group = pos[2]
    part = own.shape[0]
    for k, out in enumerate((own, *others)):
        at = pl.ds(pl.multiple_of((group ^ k) * part, 8), part)
        out[...] = keep[at] + got[at]


def assemble_kernel(pos, mine, theirs, out):
    core, group = pos[0], pos[2]
    part = mine.shape[1]
    parts = mine.shape[0]
    for source, side in ((mine, core), (theirs, 1 - core)):
        for k in range(parts):
            at = (side * parts + (group ^ k)) * part
            out[pl.ds(pl.multiple_of(at, 8), part)] = source[k]


def collect_codes(entries, chips, tabs):
    for ref, where, first in entries:

        @pl.when((where >= 0) & (where < chips))
        def _(ref=ref, where=where, first=first):
            for h in range(2):
                band = 2 * where + (first if h == 0 else 1 - first)
                codes = ref[h, ref.shape[1] - TABLE_ROWS :].astype(F32).astype(jnp.int32)
                tabs[pl.ds(band, 1)] = codes[:1]


def collect(entries, chips, g):
    frames, _, ch, columns = g.shape
    pieces = columns // LANES
    for ref, where, first in entries:

        @pl.when((where >= 0) & (where < chips))
        def _(ref=ref, where=where, first=first):
            for h in range(2):
                band = 2 * where + (first if h == 0 else 1 - first)
                for f in range(frames):
                    for r in range(2):
                        for j in range(pieces):
                            at = ((2 * f + r) * pieces + j) * ch
                            lanes = slice(LANES * j, LANES * (j + 1))
                            g[f, 2 * band + r + 1, :, lanes] = ref[h, at : at + ch]


def convolved(weights, window):
    taps = jnp.dot(weights[...], window, preferred_element_type=F32)
    size = taps.shape[0] // 3
    total = taps[size : 2 * size] + from_right(taps[:size]) + from_left(taps[2 * size :])
    return total.astype(BF16)


def spread(count_rows, row_at, me, g, weights, codes, hits, gu, sums):
    frames, _, ch, columns = g.shape
    pieces = columns // LANES

    def one_row(i, count):
        r = row_at(i)
        for f in range(frames):
            value = convolved(weights, g[f, pl.ds(r, 3)].reshape(3 * ch, columns))
            for j in range(pieces):
                for q in range(2):
                    gu[f, r, j, q] = value[q * ch : (q + 1) * ch, LANES * j : LANES * (j + 1)]
            for k in range(2 * pieces):
                lane = (2 * f + r % 2) * (2 * pieces) + k
                hits[count] = (r // 2) * LANES + lane
                count += (lax.shift_right_logical(codes[r // 2, lane], 3) == me).astype(jnp.int32)
        return count

    pairs = count_rows // 2
    count = lax.fori_loop(0, pairs, lambda p, n: one_row(2 * p + 1, one_row(2 * p, n)), 0)
    count = lax.fori_loop(2 * pairs, count_rows, one_row, count)

    def one_hit(k, _):
        hit = hits[k]
        band, lane = hit // LANES, hit % LANES
        f, block, q = lane // (4 * pieces), (lane % (4 * pieces)) // 2, lane % 2
        target = codes[band, lane] % 8
        sums[f + 1 - q, target] += gu[f, 2 * band + block // pieces, block % pieces, q].astype(F32)
        return 0

    lax.fori_loop(0, count, one_hit, 0)


def ready_rows(chip, reach, chips):
    low, high = jnp.maximum(chip - reach, 0), jnp.minimum(chip + reach, chips - 1)
    return 4 * low + (low > 0).astype(jnp.int32), 4 * high + 4 - (high < chips - 1).astype(jnp.int32)


def side(ref, reach, pos, away):
    core, chip = pos[0], pos[1]
    step = (1 - 2 * core) * reach
    return (ref, chip + step, 1 - core) if away else (ref, chip - step, core)


def stage(old, reach, chips, entries, pos, weights, sums, g, tabs, codes, hits, gu, sem):
    core, chip = pos[0], pos[1]
    me = 2 * chip + core
    collect_codes(entries, chips, tabs)
    copy = pltpu.make_async_copy(tabs, codes, sem)
    copy.start()
    frames, rows, ch, columns = g.shape
    zero = jnp.zeros((ch, columns), BF16)
    for f in range(frames):
        g[f, 0] = zero
        g[f, rows - 1] = zero
    collect(entries, chips, g)
    copy.wait()
    low, high = ready_rows(chip, reach, chips)
    if old is None:
        spread(high - low, lambda i: low + i, me, g, weights, codes, hits, gu, sums)
    else:
        old_low, old_high = ready_rows(chip, old, chips)
        below = old_low - low
        spread(
            below + high - old_high,
            lambda i: jnp.where(i < below, low + i, old_high + i - below),
            me, g, weights, codes, hits, gu, sums,
        )


def first_stage_kernel(chips, pos, own, wa, sums, *work):
    sums[...] = jnp.zeros(sums.shape, F32)
    stage(None, 0, chips, [side(own, 0, pos, False)], pos, wa, sums, *work)


def middle_stage_kernel(chips, pos, own, near1, near2, far1, far2, wa, sums_in, sums, *work):
    sums[...] = sums_in[...]
    entries = [side(own, 0, pos, False), side(near1, 1, pos, False), side(near2, 2, pos, False)]
    entries += [side(far1, 1, pos, True), side(far2, 2, pos, True)]
    stage(0, 2, chips, entries, pos, wa, sums, *work)


def final_stage_kernel(chips, pos, near2, far2, near3, far3, wa, sums_in, passed, local, sums, *work):
    sums[...] = sums_in[...]
    entries = [side(near2, 2, pos, False), side(far2, 2, pos, True)]
    entries += [side(near3, 3, pos, False), side(far3, 3, pos, True)]
    stage(2, 3, chips, entries, pos, wa, sums, *work)
    for s in range(2):
        passed[s] = sums[s].astype(BF16)
    local[...] = sums[2]


def features_kernel(pos, own, near, wf, feat, rows4):
    core = pos[0]
    frames, _, ch, columns = feat.shape
    pieces = columns // LANES
    for f in range(frames):
        for j in range(pieces):
            lanes = slice(LANES * j, LANES * (j + 1))

            def at(r):
                return pl.ds(pl.multiple_of(((2 * f + r) * pieces + j) * ch, ch), ch)

            rows4[3 * core, :, lanes] = near[1, at(1 - core)]
            rows4[3 * (1 - core), :, lanes] = own[1, at(core)]
            for r in range(2):
                rows4[1 + r, :, lanes] = own[0, at(r)]
        for r in range(2):
            feat[f, r] = convolved(wf, rows4[r : r + 3].reshape(3 * ch, columns))


def last_kernel(passed, local, prop):
    ch = local.shape[1]
    pieces = prop.shape[3] // LANES
    for s in range(2):
        for b in range(2 * pieces):
            j = b % pieces
            value = passed[s, b]
            if s == 0:
                value = (value.astype(F32) + local[b]).astype(BF16)
            prop[s, b // pieces, :, LANES * j : LANES * (j + 1)] = value


def total_over(parts):
    first = parts[0]
    for part in parts[1:]:
        first = first + part
    return first


def few_bands(features, aligned, cotangent, weight, src_tile, src_blk):
    frames, channels, height, columns = features.shape
    inner = channels + aligned.shape[1]
    tiles = lax.axis_size("tile")
    groups = lax.axis_size("tm")
    chips = tiles // 2
    tile = lax.axis_index("tile")
    group = lax.axis_index("tm")
    core = tile % 2
    pos = jnp.stack([core, tile // 2, group]).astype(jnp.int32)

    cores = [(i, i ^ 1) for i in range(tiles)]
    joints = [(2 * z + 1, 2 * z + 2) for z in range(chips - 1)]
    joints += [(b, a) for a, b in joints]

    def hop(k):
        route = []
        for z in range(k, chips - 1):
            route += [(2 * z, 2 * z + 2), (2 * (chips - 1 - z) + 1, 2 * (chips - 1 - z) - 1)]
        return route

    def to_tile(block, route):
        return lax.ppermute(block, "tile", route)

    def to_group(block, route):
        return lax.ppermute(block, "tm", route)

    pieces = columns // LANES
    u = jnp.transpose(jnp.concatenate((features, aligned), axis=1), (0, 2, 1, 3))
    u = after(u)
    rout = to_tile(lax.dynamic_index_in_dim(u, core, 1, keepdims=False), joints)
    rin = to_tile(lax.dynamic_index_in_dim(u, 1 - core, 1, keepdims=False), cores)
    cot = jnp.transpose(cotangent, (0, 2, 1, 3))
    w3 = weight.reshape(3, 3 * channels, inner)
    codes = (src_tile * 8 + src_blk).reshape(1, -1).astype(BF16)
    tab = jnp.pad(codes, ((0, TABLE_ROWS - 1), (0, LANES - codes.shape[1])))

    halo = pltpu.VMEM((2, frames, inner, columns), BF16)
    msg_rows = 2 * frames * pieces * channels + TABLE_ROWS
    (msg,) = call(
        forward_kernel,
        [jax.ShapeDtypeStruct((msg_rows, LANES), BF16)],
        (pos, u, rin, rout, cot, w3, tab),
        1,
        [halo],
    )

    half_shape = jax.ShapeDtypeStruct((9 * channels // 2, inner), F32)
    weight_shapes = [
        jax.ShapeDtypeStruct((3 * n, 3 * channels), BF16) for n in (inner - channels, channels)
    ]
    swaps = [[(i, i ^ k) for i in range(groups)] for k in range(groups)]
    turns = [[(2 * z + c, 2 * (z ^ k) + c) for z in range(chips) for c in range(2)] for k in range(chips)]
    bands = 2 * chips
    sums_shape = (3, 2 * pieces, channels, LANES)
    work = [
        pltpu.VMEM((frames, 2 * bands + 2, channels, columns), BF16),
        pltpu.VMEM((bands, LANES), jnp.int32),
        pltpu.SMEM((bands, LANES), jnp.int32),
        pltpu.SMEM((4 * pieces * bands + 1,), jnp.int32),
        pltpu.VMEM((frames, 2 * bands, pieces, 2, channels, LANES), BF16),
        pltpu.SemaphoreType.DMA,
    ]

    other = to_tile(msg, cores)
    own = jnp.stack((msg, other))
    near1 = to_tile(own, hop(0))
    keep, send, wa, wf = call(
        taps_kernel,
        [half_shape, half_shape, *weight_shapes],
        (pos, u, rin, rout, after(msg, own), w3),
        1,
        [
            halo,
            pltpu.VMEM((9 * channels, inner), F32),
            pltpu.VMEM((frames, 2, 3 * channels, columns), BF16),
        ],
        micros=0.0,
    )
    got = to_tile(send, cores)
    part_rows = 9 * channels // (2 * groups)
    part_shape = jax.ShapeDtypeStruct((part_rows, inner), F32)
    shares = call(shares_kernel, [part_shape] * groups, (pos, keep, got), 1, micros=0.0)

    (sums,) = call(
        lambda *refs: first_stage_kernel(chips, *refs),
        [jax.ShapeDtypeStruct(sums_shape, F32)],
        (pos, own, wa),
        1,
        work,
        micros=0.0,
    )
    near1 = after(near1, sums, *shares)
    near2 = to_tile(near1, hop(1))
    far1 = to_tile(near1, cores)
    shares = [after(x, far1) for x in shares]
    share = total_over([shares[0]] + [to_group(shares[k], swaps[k]) for k in range(1, groups)])
    pixels = frames * groups * height * tiles * columns
    near2 = after(near2, share)
    near3 = to_tile(near2, hop(2))
    far = [far1, to_tile(near2, cores)]
    share = after(share, *far)
    share = total_over([share] + [to_tile(share, turns[k]) for k in range(1, chips)])
    share = share * (1.0 / math.sqrt(pixels))
    (sums,) = call(
        lambda *refs: middle_stage_kernel(chips, *refs),
        [jax.ShapeDtypeStruct(sums_shape, F32)],
        (pos, own, near1, near2, *far, wa, sums),
        1,
        work,
        micros=2.0,
    )
    share = after(share, sums)
    near3 = after(near3, share, sums)
    far3 = to_tile(near3, cores)
    passed, local = call(
        lambda *refs: final_stage_kernel(chips, *refs),
        [jax.ShapeDtypeStruct((2, *sums_shape[1:]), BF16), jax.ShapeDtypeStruct(sums_shape[1:], F32)],
        (pos, near2, far[1], near3, far3, wa, sums),
        1,
        [pltpu.VMEM(sums_shape, F32)] + work,
        micros=0.0,
    )
    mine = jnp.stack([share] + [to_group(share, swaps[k]) for k in range(1, groups)])
    (feat,) = call(
        features_kernel,
        [jax.ShapeDtypeStruct((frames, 2, channels, columns), BF16)],
        (pos, after(own, passed), near1, wf),
        1,
        [pltpu.VMEM((4, channels, columns), BF16)],
    )
    passed = to_group(passed, [(m + 1, m) for m in range(groups - 1)])
    theirs = to_tile(mine, cores)
    (grad_weight,) = call(
        assemble_kernel, [jax.ShapeDtypeStruct((9 * channels, inner), F32)], (pos, mine, theirs), 1
    )

    (prop,) = call(
        last_kernel, [jax.ShapeDtypeStruct((2, 2, channels, columns), BF16)], (passed, local), 0
    )
    return (
        grad_weight.reshape(9, channels, inner),
        jnp.transpose(feat, (0, 2, 1, 3)),
        jnp.transpose(prop, (0, 2, 1, 3)),
    )


def with_halo(cells, sides, width):
    for axis, dim in sides:
        count = lax.axis_size(axis)
        ends = count - 1
        head = lax.slice_in_dim(cells, 0, width, axis=dim)
        tail = lax.slice_in_dim(cells, cells.shape[dim] - width, cells.shape[dim], axis=dim)
        cells = jnp.concatenate(
            [
                lax.ppermute(tail, axis, [(i, (i + 1) % count) for i in range(ends)]),
                cells,
                lax.ppermute(head, axis, [((i + 1) % count, i) for i in range(ends)]),
            ],
            axis=dim,
        )
    return cells


def passed_along(block, axis, distance):
    devices = range(lax.axis_size(axis))
    route = [(i - distance, i) for i in devices if i - distance in devices]
    return lax.ppermute(block, axis, route)


def pad_columns(values):
    return jnp.pad(values, ((0, 0), (0, 0), (0, 0), (1, 1)))


def conv_forward(weight, padded_input, height):
    columns = padded_input.shape[3] - 2
    summed = jnp.zeros((padded_input.shape[0], weight.shape[1], height, columns), jnp.float32)
    for row_tap in range(3):
        for col_tap in range(3):
            window = padded_input[:, :, row_tap : row_tap + height, col_tap : col_tap + columns]
            summed = summed + jnp.einsum(
                "oi,firc->forc",
                weight[3 * row_tap + col_tap],
                window,
                preferred_element_type=jnp.float32,
            )
    return summed


def conv_transpose(weight, padded_input, height):
    columns = padded_input.shape[3] - 2
    summed = jnp.zeros((padded_input.shape[0], weight.shape[2], height, columns), jnp.float32)
    for row_tap in range(3):
        for col_tap in range(3):
            window = padded_input[
                :, :, 2 - row_tap : 2 - row_tap + height, 2 - col_tap : 2 - col_tap + columns
            ]
            summed = summed + jnp.einsum(
                "oi,forc->firc",
                weight[3 * row_tap + col_tap],
                window,
                preferred_element_type=jnp.float32,
            )
    return summed.astype(jnp.bfloat16)


def weight_grad(padded_input, cot_pre):
    height = cot_pre.shape[2]
    columns = cot_pre.shape[3]
    term_list = []
    for row_tap in range(3):
        for col_tap in range(3):
            window = padded_input[:, :, row_tap : row_tap + height, col_tap : col_tap + columns]
            term_list.append(
                jnp.einsum("forc,firc->oi", cot_pre, window, preferred_element_type=jnp.float32)
            )
    return jnp.stack(term_list)


def build_slots(aligned_grad, tiles, blocks, tile_count, capacity):
    frames, stacked, height, columns = aligned_grad.shape
    block_count = tiles.shape[1]
    pixels = height * columns // block_count
    pieces = aligned_grad.reshape(frames, 2, stacked // 2, block_count, pixels)
    row_ids = jnp.arange(2 * block_count, dtype=jnp.int32)
    destination = jnp.swapaxes(tiles, 1, 2).reshape(frames, 2 * block_count)
    target_code = (
        jnp.swapaxes(blocks, 1, 2).reshape(frames, 2 * block_count)
        + (row_ids // block_count * block_count)[None, :]
    )
    tile_hit_count = (
        destination[:, :, None] == jnp.arange(tile_count, dtype=jnp.int32)[None, None, :]
    ).astype(jnp.int32)
    earlier = jnp.cumsum(tile_hit_count, axis=1) - tile_hit_count
    slot_ids = destination * capacity + jnp.sum(tile_hit_count * earlier, axis=2)
    source_selector = (
        slot_ids[:, None, :] == jnp.arange(tile_count * capacity, dtype=jnp.int32)[None, :, None]
    ).astype(jnp.bfloat16)
    target_onehot = (target_code[:, :, None] == row_ids[None, None, :]).astype(jnp.bfloat16)
    placing = jnp.einsum(
        "anu,auo->ano", source_selector, target_onehot, preferred_element_type=jnp.float32
    ).astype(jnp.bfloat16)
    select_split = source_selector.reshape(frames, tile_count * capacity, 2, block_count)
    payload = jnp.einsum(
        "fsob,focbp->fscp", select_split, pieces, preferred_element_type=jnp.float32
    ).astype(jnp.bfloat16)
    return (payload, placing)


def place_blocks(received):
    payload, placing = received
    return jnp.einsum("fsb,fscp->fcbp", placing, payload, preferred_element_type=jnp.float32)


def deliver(aligned_grad, tiles, blocks, tile_count, capacity):
    payload, placing = build_slots(aligned_grad, tiles, blocks, tile_count, capacity)
    return place_blocks(
        (
            lax.all_to_all(payload, "tile", split_axis=1, concat_axis=1, tiled=True),
            lax.all_to_all(placing, "tile", split_axis=1, concat_axis=1, tiled=True),
        )
    )


def many_bands(features, aligned, cotangent, weight, src_tile, src_blk):
    frames, channels, height, columns = features.shape
    inputs = jnp.concatenate((features, aligned), axis=1)
    padded_in = pad_columns(with_halo(inputs, (("tile", 2),), 1))
    preact = conv_forward(weight, padded_in, height)
    cot_pre = (cotangent * act_slope(preact)).astype(jnp.bfloat16)
    padded_cot = pad_columns(with_halo(cot_pre, (("tile", 2),), 1))
    tile_count = lax.axis_size("tile")
    block_count = src_tile.shape[1]
    capacity = max(2, (4 * block_count + tile_count - 1) // tile_count)
    input_grad = conv_transpose(weight, padded_cot, height)
    local_weight = weight_grad(padded_in, cot_pre)
    feat_grad = input_grad[:, :channels]
    aligned_grad = input_grad[:, channels:]
    arrived = deliver(aligned_grad, src_tile, src_blk, tile_count, capacity)
    landed = arrived.reshape(frames, channels, 2, height, columns)
    extended = jnp.pad(landed[:, :, 0], ((1, 1), (0, 0), (0, 0), (0, 0))) + jnp.pad(
        landed[:, :, 1], ((0, 2), (0, 0), (0, 0), (0, 0))
    )
    arriving = passed_along(extended[:2], "tm", -1)
    resident = extended[2:]
    resident = jnp.concatenate((resident[: frames - 2], resident + arriving), axis=0)
    total_weight = lax.psum(local_weight, ("tm", "tile"))
    pixels = frames * lax.axis_size("tm") * height * tile_count * columns
    grad_weight = total_weight * (1.0 / math.sqrt(pixels))
    return (grad_weight, feat_grad, resident.astype(jnp.bfloat16))


def solution(mesh):
    in_specs = (
        P("tm", None, "tile", None),
        P("tm", None, "tile", None),
        P("tm", None, "tile", None),
        P(),
        P("tm", "tile", None),
        P("tm", "tile", None),
    )
    out_specs = (P(), P("tm", None, "tile", None), P("tm", None, "tile", None))
    few = mesh.shape["tile"] == 8 and mesh.shape["tm"] == 4
    body = few_bands if few else many_bands
    return jax.shard_map(body, mesh=mesh, in_specs=in_specs, out_specs=out_specs, check_vma=False)
```

```python
import math

import jax
import jax.numpy as jnp
from jax import lax
from jax.experimental import pallas as pl
from jax.experimental.pallas import tpu as pltpu
from jax.sharding import PartitionSpec as P

F32 = jnp.float32
BF16 = jnp.bfloat16


def act_slope(preact):
    return 0.1 + 0.9 * jax.nn.sigmoid(preact)


TABLE_ROWS = 16
LANES = 128


def full(memory_space=pltpu.VMEM):
    return pl.BlockSpec(memory_space=memory_space)


def call(kernel, out_shapes, args, scalars, scratch=(), micros=0.0):
    specs = [full(pltpu.SMEM)] * scalars + [full()] * (len(args) - scalars)
    return pl.pallas_call(
        kernel,
        out_shape=out_shapes,
        in_specs=specs,
        out_specs=[full()] * len(out_shapes),
        scratch_shapes=list(scratch),
        cost_estimate=pl.CostEstimate(flops=int(micros * 1e9), bytes_accessed=0, transcendentals=0),
        compiler_params=pltpu.CompilerParams(vmem_limit_bytes=24 << 20),
    )(*args)


def after(value, *others):
    return lax.optimization_barrier((value, *others))[0]


def from_left(values):
    lane = lax.broadcasted_iota(jnp.int32, values.shape, 1)
    return jnp.where(lane == 0, 0.0, pltpu.roll(values, 1, 1))


def from_right(values):
    columns = values.shape[1]
    lane = lax.broadcasted_iota(jnp.int32, values.shape, 1)
    return jnp.where(lane == columns - 1, 0.0, pltpu.roll(values, columns - 1, 1))


def taps_of(row):
    wide = row.astype(F32)
    return (from_right(wide).astype(BF16), row, from_left(wide).astype(BF16))


def forward_kernel(pos, u, rin, rout, cot, wide, tab, msg, halo):
    core = pos[0]
    frames, _, ch, columns = cot.shape
    pieces = columns // LANES
    halo[core] = rout[...]
    halo[1 - core] = rin[...]
    for f in range(frames):
        rows = (halo.at[0, f], u.at[f, 0], u.at[f, 1], halo.at[1, f])
        for r in range(2):
            window = jnp.concatenate([row[...] for row in rows[r : r + 3]], axis=0)
            taps = jnp.dot(wide[...], window, preferred_element_type=F32)
            z = taps[ch : 2 * ch] + from_left(taps[:ch]) + from_right(taps[2 * ch :])
            g = (cot[f, r].astype(F32) * act_slope(z)).astype(BF16)
            for j in range(pieces):
                at = ((2 * f + r) * pieces + j) * ch
                msg[at : at + ch] = g[:, LANES * j : LANES * (j + 1)]
    msg[2 * frames * pieces * ch :] = tab[...]


def taps_kernel(pos, u, rin, rout, msg, w3, keep, send, wa, wf, halo, total, g3):
    core = pos[0]
    frames, _, size, columns = g3.shape
    ch = size // 3
    pieces = columns // LANES
    half = keep.shape[0]
    halo[core] = rout[...]
    halo[1 - core] = rin[...]
    for f in range(frames):
        for r in range(2):
            at = (2 * f + r) * pieces * ch
            row = jnp.concatenate([msg[at + j * ch : at + (j + 1) * ch] for j in range(pieces)], axis=1)
            for k, part in enumerate(taps_of(row)):
                g3[f, r, k * ch : (k + 1) * ch] = part
    for ky in range(3):
        acc = jnp.zeros((size, u.shape[2]), F32)
        for f in range(u.shape[0]):
            rows = (halo.at[0, f], u.at[f, 0], u.at[f, 1], halo.at[1, f])
            for r in range(2):
                acc += lax.dot_general(
                    g3[f, r], rows[r + ky][...], (((1,), (1,)), ((), ())), preferred_element_type=F32
                )
        total[ky * size : (ky + 1) * size] = acc
    keep[...] = total[pl.ds(pl.multiple_of(core * half, 8), half)]
    send[...] = total[pl.ds(pl.multiple_of((1 - core) * half, 8), half)]
    for kx in range(3):
        rows = [w3[ky, kx * ch : (kx + 1) * ch] for ky in (2, 1, 0)]
        turned = jnp.transpose(jnp.concatenate(rows, axis=0).astype(F32)).astype(BF16)
        wf[kx * ch : (kx + 1) * ch] = turned[:ch]
        wa[2 * kx * ch : 2 * (kx + 1) * ch] = turned[ch:]


def shares_kernel(pos, keep, got, own, *others):
    group = pos[2]
    part = own.shape[0]
    for k, out in enumerate((own, *others)):
        at = pl.ds(pl.multiple_of((group ^ k) * part, 8), part)
        out[...] = keep[at] + got[at]


def assemble_kernel(pos, mine, theirs, out):
    core, group = pos[0], pos[2]
    part = mine.shape[1]
    parts = mine.shape[0]
    for source, side in ((mine, core), (theirs, 1 - core)):
        for k in range(parts):
            at = (side * parts + (group ^ k)) * part
            out[pl.ds(pl.multiple_of(at, 8), part)] = source[k]


def collect_codes(entries, chips, tabs):
    for ref, where, first in entries:

        @pl.when((where >= 0) & (where < chips))
        def _(ref=ref, where=where, first=first):
            for h in range(2):
                band = 2 * where + (first if h == 0 else 1 - first)
                codes = ref[h, ref.shape[1] - TABLE_ROWS :].astype(F32).astype(jnp.int32)
                tabs[pl.ds(band, 1)] = codes[:1]


def collect(entries, chips, g):
    frames, _, ch, columns = g.shape
    pieces = columns // LANES
    for ref, where, first in entries:

        @pl.when((where >= 0) & (where < chips))
        def _(ref=ref, where=where, first=first):
            for h in range(2):
                band = 2 * where + (first if h == 0 else 1 - first)
                for f in range(frames):
                    for r in range(2):
                        for j in range(pieces):
                            at = ((2 * f + r) * pieces + j) * ch
                            lanes = slice(LANES * j, LANES * (j + 1))
                            g[f, 2 * band + r + 1, :, lanes] = ref[h, at : at + ch]


def convolved(weights, window):
    taps = jnp.dot(weights[...], window, preferred_element_type=F32)
    size = taps.shape[0] // 3
    total = taps[size : 2 * size] + from_right(taps[:size]) + from_left(taps[2 * size :])
    return total.astype(BF16)


def spread(count_rows, row_at, me, g, weights, codes, hits, gu, sums):
    frames, _, ch, columns = g.shape
    pieces = columns // LANES

    def one_row(i, count):
        r = row_at(i)
        for f in range(frames):
            value = convolved(weights, g[f, pl.ds(r, 3)].reshape(3 * ch, columns))
            for j in range(pieces):
                for q in range(2):
                    gu[f, r, j, q] = value[q * ch : (q + 1) * ch, LANES * j : LANES * (j + 1)]
            for k in range(2 * pieces):
                lane = (2 * f + r % 2) * (2 * pieces) + k
                hits[count] = (r // 2) * LANES + lane
                count += (lax.shift_right_logical(codes[r // 2, lane], 3) == me).astype(jnp.int32)
        return count

    pairs = count_rows // 2
    count = lax.fori_loop(0, pairs, lambda p, n: one_row(2 * p + 1, one_row(2 * p, n)), 0)
    count = lax.fori_loop(2 * pairs, count_rows, one_row, count)

    def one_hit(k, _):
        hit = hits[k]
        band, lane = hit // LANES, hit % LANES
        f, block, q = lane // (4 * pieces), (lane % (4 * pieces)) // 2, lane % 2
        target = codes[band, lane] % 8
        sums[f + 1 - q, target] += gu[f, 2 * band + block // pieces, block % pieces, q].astype(F32)
        return 0

    lax.fori_loop(0, count, one_hit, 0)


def ready_rows(chip, reach, chips):
    low, high = jnp.maximum(chip - reach, 0), jnp.minimum(chip + reach, chips - 1)
    return 4 * low + (low > 0).astype(jnp.int32), 4 * high + 4 - (high < chips - 1).astype(jnp.int32)


def side(ref, reach, pos, away):
    core, chip = pos[0], pos[1]
    step = (1 - 2 * core) * reach
    return (ref, chip + step, 1 - core) if away else (ref, chip - step, core)


def stage(old, reach, chips, entries, pos, weights, sums, g, tabs, codes, hits, gu, sem):
    core, chip = pos[0], pos[1]
    me = 2 * chip + core
    collect_codes(entries, chips, tabs)
    copy = pltpu.make_async_copy(tabs, codes, sem)
    copy.start()
    frames, rows, ch, columns = g.shape
    zero = jnp.zeros((ch, columns), BF16)
    for f in range(frames):
        g[f, 0] = zero
        g[f, rows - 1] = zero
    collect(entries, chips, g)
    copy.wait()
    low, high = ready_rows(chip, reach, chips)
    if old is None:
        spread(high - low, lambda i: low + i, me, g, weights, codes, hits, gu, sums)
    else:
        old_low, old_high = ready_rows(chip, old, chips)
        below = old_low - low
        spread(
            below + high - old_high,
            lambda i: jnp.where(i < below, low + i, old_high + i - below),
            me, g, weights, codes, hits, gu, sums,
        )


def first_stage_kernel(chips, pos, own, wa, sums, *work):
    sums[...] = jnp.zeros(sums.shape, F32)
    stage(None, 0, chips, [side(own, 0, pos, False)], pos, wa, sums, *work)


def middle_stage_kernel(chips, pos, own, near1, near2, far1, far2, wa, sums_in, sums, *work):
    sums[...] = sums_in[...]
    entries = [side(own, 0, pos, False), side(near1, 1, pos, False), side(near2, 2, pos, False)]
    entries += [side(far1, 1, pos, True), side(far2, 2, pos, True)]
    stage(0, 2, chips, entries, pos, wa, sums, *work)


def final_stage_kernel(chips, pos, near2, far2, near3, far3, wa, sums_in, passed, local, sums, *work):
    sums[...] = sums_in[...]
    entries = [side(near2, 2, pos, False), side(far2, 2, pos, True)]
    entries += [side(near3, 3, pos, False), side(far3, 3, pos, True)]
    stage(2, 3, chips, entries, pos, wa, sums, *work)
    for s in range(2):
        passed[s] = sums[s].astype(BF16)
    local[...] = sums[2]


def features_kernel(pos, own, near, wf, feat, rows4):
    core = pos[0]
    frames, _, ch, columns = feat.shape
    pieces = columns // LANES
    for f in range(frames):
        for j in range(pieces):
            lanes = slice(LANES * j, LANES * (j + 1))

            def at(r):
                return pl.ds(pl.multiple_of(((2 * f + r) * pieces + j) * ch, ch), ch)

            rows4[3 * core, :, lanes] = near[1, at(1 - core)]
            rows4[3 * (1 - core), :, lanes] = own[1, at(core)]
            for r in range(2):
                rows4[1 + r, :, lanes] = own[0, at(r)]
        for r in range(2):
            feat[f, r] = convolved(wf, rows4[r : r + 3].reshape(3 * ch, columns))


def last_kernel(passed, local, prop):
    ch = local.shape[1]
    pieces = prop.shape[3] // LANES
    for s in range(2):
        for b in range(2 * pieces):
            j = b % pieces
            value = passed[s, b]
            if s == 0:
                value = (value.astype(F32) + local[b]).astype(BF16)
            prop[s, b // pieces, :, LANES * j : LANES * (j + 1)] = value


def total_over(parts):
    first = parts[0]
    for part in parts[1:]:
        first = first + part
    return first


def few_bands(features, aligned, cotangent, weight, src_tile, src_blk):
    frames, channels, height, columns = features.shape
    inner = channels + aligned.shape[1]
    tiles = lax.axis_size("tile")
    groups = lax.axis_size("tm")
    chips = tiles // 2
    tile = lax.axis_index("tile")
    group = lax.axis_index("tm")
    core = tile % 2
    pos = jnp.stack([core, tile // 2, group]).astype(jnp.int32)

    cores = [(i, i ^ 1) for i in range(tiles)]
    joints = [(2 * z + 1, 2 * z + 2) for z in range(chips - 1)]
    joints += [(b, a) for a, b in joints]

    def hop(k):
        route = []
        for z in range(k, chips - 1):
            route += [(2 * z, 2 * z + 2), (2 * (chips - 1 - z) + 1, 2 * (chips - 1 - z) - 1)]
        return route

    def to_tile(block, route):
        return lax.ppermute(block, "tile", route)

    def to_group(block, route):
        return lax.ppermute(block, "tm", route)

    pieces = columns // LANES
    u = jnp.transpose(jnp.concatenate((features, aligned), axis=1), (0, 2, 1, 3))
    u = after(u)
    rout = to_tile(lax.dynamic_index_in_dim(u, core, 1, keepdims=False), joints)
    rin = to_tile(lax.dynamic_index_in_dim(u, 1 - core, 1, keepdims=False), cores)
    cot = jnp.transpose(cotangent, (0, 2, 1, 3))
    w3 = weight.reshape(3, 3 * channels, inner)
    wide = jnp.transpose(w3, (1, 0, 2)).reshape(3 * channels, 3 * inner)
    codes = (src_tile * 8 + src_blk).reshape(1, -1).astype(BF16)
    tab = jnp.pad(codes, ((0, TABLE_ROWS - 1), (0, LANES - codes.shape[1])))

    halo = pltpu.VMEM((2, frames, inner, columns), BF16)
    msg_rows = 2 * frames * pieces * channels + TABLE_ROWS
    (msg,) = call(
        forward_kernel,
        [jax.ShapeDtypeStruct((msg_rows, LANES), BF16)],
        (pos, u, rin, rout, cot, wide, tab),
        1,
        [halo],
    )

    half_shape = jax.ShapeDtypeStruct((9 * channels // 2, inner), F32)
    weight_shapes = [
        jax.ShapeDtypeStruct((3 * n, 3 * channels), BF16) for n in (inner - channels, channels)
    ]
    swaps = [[(i, i ^ k) for i in range(groups)] for k in range(groups)]
    turns = [[(2 * z + c, 2 * (z ^ k) + c) for z in range(chips) for c in range(2)] for k in range(chips)]
    bands = 2 * chips
    sums_shape = (3, 2 * pieces, channels, LANES)
    work = [
        pltpu.VMEM((frames, 2 * bands + 2, channels, columns), BF16),
        pltpu.VMEM((bands, LANES), jnp.int32),
        pltpu.SMEM((bands, LANES), jnp.int32),
        pltpu.SMEM((4 * pieces * bands + 1,), jnp.int32),
        pltpu.VMEM((frames, 2 * bands, pieces, 2, channels, LANES), BF16),
        pltpu.SemaphoreType.DMA,
    ]

    other = to_tile(msg, cores)
    own = jnp.stack((msg, other))
    near1 = to_tile(own, hop(0))
    keep, send, wa, wf = call(
        taps_kernel,
        [half_shape, half_shape, *weight_shapes],
        (pos, u, rin, rout, after(msg, own), w3),
        1,
        [
            halo,
            pltpu.VMEM((9 * channels, inner), F32),
            pltpu.VMEM((frames, 2, 3 * channels, columns), BF16),
        ],
        micros=0.0,
    )
    got = to_tile(send, cores)
    part_rows = 9 * channels // (2 * groups)
    part_shape = jax.ShapeDtypeStruct((part_rows, inner), F32)
    shares = call(shares_kernel, [part_shape] * groups, (pos, keep, got), 1, micros=0.0)

    (sums,) = call(
        lambda *refs: first_stage_kernel(chips, *refs),
        [jax.ShapeDtypeStruct(sums_shape, F32)],
        (pos, own, wa),
        1,
        work,
        micros=0.0,
    )
    near1 = after(near1, sums, *shares)
    near2 = to_tile(near1, hop(1))
    far1 = to_tile(near1, cores)
    shares = [after(x, far1) for x in shares]
    share = total_over([shares[0]] + [to_group(shares[k], swaps[k]) for k in range(1, groups)])
    pixels = frames * groups * height * tiles * columns
    near2 = after(near2, share)
    near3 = to_tile(near2, hop(2))
    far = [far1, to_tile(near2, cores)]
    share = after(share, *far)
    share = total_over([share] + [to_tile(share, turns[k]) for k in range(1, chips)])
    share = share * (1.0 / math.sqrt(pixels))
    (sums,) = call(
        lambda *refs: middle_stage_kernel(chips, *refs),
        [jax.ShapeDtypeStruct(sums_shape, F32)],
        (pos, own, near1, near2, *far, wa, sums),
        1,
        work,
        micros=2.0,
    )
    share = after(share, sums)
    near3 = after(near3, share, sums)
    far3 = to_tile(near3, cores)
    passed, local = call(
        lambda *refs: final_stage_kernel(chips, *refs),
        [jax.ShapeDtypeStruct((2, *sums_shape[1:]), BF16), jax.ShapeDtypeStruct(sums_shape[1:], F32)],
        (pos, near2, far[1], near3, far3, wa, sums),
        1,
        [pltpu.VMEM(sums_shape, F32)] + work,
        micros=0.0,
    )
    mine = jnp.stack([share] + [to_group(share, swaps[k]) for k in range(1, groups)])
    (feat,) = call(
        features_kernel,
        [jax.ShapeDtypeStruct((frames, 2, channels, columns), BF16)],
        (pos, after(own, passed), near1, wf),
        1,
        [pltpu.VMEM((4, channels, columns), BF16)],
    )
    passed = to_group(passed, [(m + 1, m) for m in range(groups - 1)])
    theirs = to_tile(mine, cores)
    (grad_weight,) = call(
        assemble_kernel, [jax.ShapeDtypeStruct((9 * channels, inner), F32)], (pos, mine, theirs), 1
    )

    (prop,) = call(
        last_kernel, [jax.ShapeDtypeStruct((2, 2, channels, columns), BF16)], (passed, local), 0
    )
    return (
        grad_weight.reshape(9, channels, inner),
        jnp.transpose(feat, (0, 2, 1, 3)),
        jnp.transpose(prop, (0, 2, 1, 3)),
    )


def with_halo(cells, sides, width):
    for axis, dim in sides:
        count = lax.axis_size(axis)
        ends = count - 1
        head = lax.slice_in_dim(cells, 0, width, axis=dim)
        tail = lax.slice_in_dim(cells, cells.shape[dim] - width, cells.shape[dim], axis=dim)
        cells = jnp.concatenate(
            [
                lax.ppermute(tail, axis, [(i, (i + 1) % count) for i in range(ends)]),
                cells,
                lax.ppermute(head, axis, [((i + 1) % count, i) for i in range(ends)]),
            ],
            axis=dim,
        )
    return cells


def passed_along(block, axis, distance):
    devices = range(lax.axis_size(axis))
    route = [(i - distance, i) for i in devices if i - distance in devices]
    return lax.ppermute(block, axis, route)


def pad_columns(values):
    return jnp.pad(values, ((0, 0), (0, 0), (0, 0), (1, 1)))


def conv_forward(weight, padded_input, height):
    columns = padded_input.shape[3] - 2
    summed = jnp.zeros((padded_input.shape[0], weight.shape[1], height, columns), jnp.float32)
    for row_tap in range(3):
        for col_tap in range(3):
            window = padded_input[:, :, row_tap : row_tap + height, col_tap : col_tap + columns]
            summed = summed + jnp.einsum(
                "oi,firc->forc",
                weight[3 * row_tap + col_tap],
                window,
                preferred_element_type=jnp.float32,
            )
    return summed


def conv_transpose(weight, padded_input, height):
    columns = padded_input.shape[3] - 2
    summed = jnp.zeros((padded_input.shape[0], weight.shape[2], height, columns), jnp.float32)
    for row_tap in range(3):
        for col_tap in range(3):
            window = padded_input[
                :, :, 2 - row_tap : 2 - row_tap + height, 2 - col_tap : 2 - col_tap + columns
            ]
            summed = summed + jnp.einsum(
                "oi,forc->firc",
                weight[3 * row_tap + col_tap],
                window,
                preferred_element_type=jnp.float32,
            )
    return summed.astype(jnp.bfloat16)


def weight_grad(padded_input, cot_pre):
    height = cot_pre.shape[2]
    columns = cot_pre.shape[3]
    term_list = []
    for row_tap in range(3):
        for col_tap in range(3):
            window = padded_input[:, :, row_tap : row_tap + height, col_tap : col_tap + columns]
            term_list.append(
                jnp.einsum("forc,firc->oi", cot_pre, window, preferred_element_type=jnp.float32)
            )
    return jnp.stack(term_list)


def build_slots(aligned_grad, tiles, blocks, tile_count, capacity):
    frames, stacked, height, columns = aligned_grad.shape
    block_count = tiles.shape[1]
    pixels = height * columns // block_count
    pieces = aligned_grad.reshape(frames, 2, stacked // 2, block_count, pixels)
    row_ids = jnp.arange(2 * block_count, dtype=jnp.int32)
    destination = jnp.swapaxes(tiles, 1, 2).reshape(frames, 2 * block_count)
    target_code = (
        jnp.swapaxes(blocks, 1, 2).reshape(frames, 2 * block_count)
        + (row_ids // block_count * block_count)[None, :]
    )
    tile_hit_count = (
        destination[:, :, None] == jnp.arange(tile_count, dtype=jnp.int32)[None, None, :]
    ).astype(jnp.int32)
    earlier = jnp.cumsum(tile_hit_count, axis=1) - tile_hit_count
    slot_ids = destination * capacity + jnp.sum(tile_hit_count * earlier, axis=2)
    source_selector = (
        slot_ids[:, None, :] == jnp.arange(tile_count * capacity, dtype=jnp.int32)[None, :, None]
    ).astype(jnp.bfloat16)
    target_onehot = (target_code[:, :, None] == row_ids[None, None, :]).astype(jnp.bfloat16)
    placing = jnp.einsum(
        "anu,auo->ano", source_selector, target_onehot, preferred_element_type=jnp.float32
    ).astype(jnp.bfloat16)
    select_split = source_selector.reshape(frames, tile_count * capacity, 2, block_count)
    payload = jnp.einsum(
        "fsob,focbp->fscp", select_split, pieces, preferred_element_type=jnp.float32
    ).astype(jnp.bfloat16)
    return (payload, placing)


def place_blocks(received):
    payload, placing = received
    return jnp.einsum("fsb,fscp->fcbp", placing, payload, preferred_element_type=jnp.float32)


def deliver(aligned_grad, tiles, blocks, tile_count, capacity):
    payload, placing = build_slots(aligned_grad, tiles, blocks, tile_count, capacity)
    return place_blocks(
        (
            lax.all_to_all(payload, "tile", split_axis=1, concat_axis=1, tiled=True),
            lax.all_to_all(placing, "tile", split_axis=1, concat_axis=1, tiled=True),
        )
    )


def many_bands(features, aligned, cotangent, weight, src_tile, src_blk):
    frames, channels, height, columns = features.shape
    inputs = jnp.concatenate((features, aligned), axis=1)
    padded_in = pad_columns(with_halo(inputs, (("tile", 2),), 1))
    preact = conv_forward(weight, padded_in, height)
    cot_pre = (cotangent * act_slope(preact)).astype(jnp.bfloat16)
    padded_cot = pad_columns(with_halo(cot_pre, (("tile", 2),), 1))
    tile_count = lax.axis_size("tile")
    block_count = src_tile.shape[1]
    capacity = max(2, (4 * block_count + tile_count - 1) // tile_count)
    input_grad = conv_transpose(weight, padded_cot, height)
    local_weight = weight_grad(padded_in, cot_pre)
    feat_grad = input_grad[:, :channels]
    aligned_grad = input_grad[:, channels:]
    arrived = deliver(aligned_grad, src_tile, src_blk, tile_count, capacity)
    landed = arrived.reshape(frames, channels, 2, height, columns)
    extended = jnp.pad(landed[:, :, 0], ((1, 1), (0, 0), (0, 0), (0, 0))) + jnp.pad(
        landed[:, :, 1], ((0, 2), (0, 0), (0, 0), (0, 0))
    )
    arriving = passed_along(extended[:2], "tm", -1)
    resident = extended[2:]
    resident = jnp.concatenate((resident[: frames - 2], resident + arriving), axis=0)
    total_weight = lax.psum(local_weight, ("tm", "tile"))
    pixels = frames * lax.axis_size("tm") * height * tile_count * columns
    grad_weight = total_weight * (1.0 / math.sqrt(pixels))
    return (grad_weight, feat_grad, resident.astype(jnp.bfloat16))


def solution(mesh):
    in_specs = (
        P("tm", None, "tile", None),
        P("tm", None, "tile", None),
        P("tm", None, "tile", None),
        P(),
        P("tm", "tile", None),
        P("tm", "tile", None),
    )
    out_specs = (P(), P("tm", None, "tile", None), P("tm", None, "tile", None))
    few = mesh.shape["tile"] == 8 and mesh.shape["tm"] == 4
    body = few_bands if few else many_bands
    return jax.shard_map(body, mesh=mesh, in_specs=in_specs, out_specs=out_specs, check_vma=False)
```
